32 devices in a mesh: groups: 2 (over y), seq: 4 (over z), rep: 2 (over x), tp: 2 (over core).
Axes of the slice: x: 2, y: 2, z: 4, core: 2. Of those that a mesh axis runs over, the one named last changes fastest.
Arguments:
- node_features: bfloat16 [4, 1024, 768], P(('groups', 'rep'), 'seq'), parts along dimension 0, may hold values from -20 to 20
- result_cotangent: bfloat16 [4, 1024, 768], P(('groups', 'rep'), 'seq', 'tp'), parts along dimension 0, may hold values from -6 to 6
- proj_weights: bfloat16 [768, 3, 768], P(None, None, 'tp'), may hold values from -2 to 2
- cluster_pairs: int32 [4, 8, 2], P(('groups', 'rep'), 'seq'), parts along dimension 0, may hold values from 0 to 7, as said below
- cluster_fill: int32 [4, 8], P(('groups', 'rep')), parts along dimension 0, may hold values from 64 to 128, as said below
- global_nodes: int32 [4, 256], P(('groups', 'rep')), parts along dimension 0, may hold values from 0 to 1023, as said below
Outputs:
- mixed_result: bfloat16 [4, 1024, 768], P(('groups', 'rep'), 'seq', 'tp'), parts along dimension 0
- grad_x: bfloat16 [4, 1024, 768], P(('groups', 'rep'), 'seq'), parts along dimension 0
- grad_w: float32 [1536, 3, 768], P(('groups', 'seq', 'rep'), None, 'tp'), parts along dimension 0
The draws below stay inside these ranges and needn't reach their ends.
There are 2 independent parts, one for each index of `groups`. The reference program is written for one: setup_inputs(seed, part) draws one part's arguments, and reference() takes and returns one part's arrays. A program takes and returns all parts, laid end to end along the dimension named above; an argument that names none is the same for every part. Nothing has to cross between parts.
Inputs may be any that keep to these rules, and one draw needn't show every extreme that they name: `cluster_pairs`: cluster c holds node slots c * 128 to c * 128 + 127 and lies on shard c // 2. Entry [c, 0] is c itself and the entries of a row differ. Over the query clusters of one shard, at most one cluster of each other shard is named, and only by one of those query clusters. `cluster_fill`: some cluster of every subgraph is full. `global_nodes`: distinct real nodes.
All inputs are finite; a program needn't handle non-finite values.
Results may differ from the reference program's by a relative error of at most 0.0045.
The reference program's roundings to bfloat16 on the way count: a program that leaves them out, or rounds other values in their place, can miss the bound.
Values may be sent and summed in bfloat16 or wider, within the bound.
No kernel may reach another device: no remote copies, remote signals or barrier semaphores. Data moves between devices by JAX's collectives and lax.ppermute only.
A program may use at most 64 MiB of HBM per device.

```python
import jax
import jax.numpy as jnp
from jax import lax

EMBED_BREADTH = 768
HEADS = 12
HDIM = 64
GROUP_VERTICES = 128
LOOKUP_GROUPS = 2
GLOBALS = 256
PER_CHIP_GROUPS = 2
ATTN_INNER_SIZE = 768
PARTITION_GROUPS = 8
PARTITION_NODES = 1024
PARTITION_TOTAL = 2


def fill_counts(key):
    key = jax.random.fold_in(key, 11)
    root_seed_handle, entire_seed_handle = jax.random.split(key)
    initial_logits = jax.random.randint(root_seed_handle, (PARTITION_TOTAL, PARTITION_GROUPS), GROUP_VERTICES // 2, GROUP_VERTICES + 1)
    global_location = jax.random.randint(entire_seed_handle, (PARTITION_TOTAL, 1), 0, PARTITION_GROUPS)
    columns = jnp.arange(PARTITION_GROUPS, dtype=jnp.int32)[None, :]
    return jnp.where(columns == global_location, GROUP_VERTICES, initial_logits).astype(jnp.int32)


def draw_cluster_fill(key, part):
    return fill_counts(key)


def draw_global_nodes(key, part):
    counts = fill_counts(key)
    key = jax.random.fold_in(key, 13)
    locations = jnp.arange(PARTITION_NODES, dtype=jnp.int32)
    real_node = (locations % GROUP_VERTICES)[None, :] < counts[:, locations // GROUP_VERTICES]
    group_sequences = jax.vmap(lambda partition_seed: jax.random.permutation(partition_seed, PARTITION_NODES))(jax.random.split(key, PARTITION_TOTAL))
    ranked = jnp.where(real_node, group_sequences.astype(jnp.int32), -1)
    chosen = lax.top_k(ranked, GLOBALS)[1]
    return chosen.astype(jnp.int32)


def draw_cluster_pairs(key, part):
    key = jax.random.fold_in(key, 7)
    partition_tally = PARTITION_GROUPS // PER_CHIP_GROUPS
    assigned_seed, caller_seed_handle, jitter_seed_handle = jax.random.split(key, 3)
    assigned_group = jax.random.randint(assigned_seed, (PARTITION_TOTAL, partition_tally, partition_tally), 0, PER_CHIP_GROUPS)
    caller_group_number = jax.random.randint(caller_seed_handle, (PARTITION_TOTAL, partition_tally, partition_tally), 0, PER_CHIP_GROUPS)
    shard_ids = jnp.arange(partition_tally, dtype=jnp.int32)
    own_ids = jnp.arange(PER_CHIP_GROUPS, dtype=jnp.int32)
    onchip_group_number = shard_ids[:, None] * PER_CHIP_GROUPS + own_ids[None, :]
    entire_extent = (PARTITION_TOTAL, partition_tally, PER_CHIP_GROUPS, PER_CHIP_GROUPS)
    local_cand = jnp.broadcast_to(onchip_group_number[None, :, None, :], entire_extent)
    local_ok = jnp.broadcast_to((own_ids[:, None] != own_ids[None, :])[None, None], entire_extent)
    remote_ids = shard_ids[None, None, :] * PER_CHIP_GROUPS + assigned_group
    foreign_tile_extent = (PARTITION_TOTAL, partition_tally, PER_CHIP_GROUPS, partition_tally)
    remote_cand = jnp.broadcast_to(remote_ids[:, :, None, :], foreign_tile_extent)
    remote_ok = (shard_ids[None, :, None, None] != shard_ids[None, None, None, :]) & (caller_group_number[:, :, None, :] == own_ids[None, None, :, None])
    candidates = jnp.concatenate([local_cand, remote_cand], -1)
    allowed = jnp.concatenate([local_ok, remote_ok], -1)
    option_set_length = PER_CHIP_GROUPS + partition_tally
    stochastic_jitter = jax.random.randint(jitter_seed_handle, (PARTITION_TOTAL, partition_tally, PER_CHIP_GROUPS, option_set_length), 0, 4096)
    extra_logit_lift = jnp.concatenate([jnp.zeros((PER_CHIP_GROUPS,), jnp.int32), jnp.full((partition_tally,), 4096, jnp.int32)])
    group_preference = (stochastic_jitter + extra_logit_lift) * option_set_length + jnp.arange(option_set_length, dtype=jnp.int32)
    group_preference = jnp.where(allowed, group_preference, -1)
    picked_index = lax.top_k(group_preference, LOOKUP_GROUPS - 1)[1]
    selected_groups = jnp.take_along_axis(candidates, picked_index, -1)
    own_group_number = jnp.broadcast_to(onchip_group_number[None, :, :, None], (PARTITION_TOTAL, partition_tally, PER_CHIP_GROUPS, 1))
    return jnp.concatenate([own_group_number, selected_groups], -1).reshape(PARTITION_TOTAL, PARTITION_GROUPS, LOOKUP_GROUPS).astype(jnp.int32)


def draw_node_features(key, part):
    key = jax.random.fold_in(key, 3)
    root_seed_handle = jax.random.fold_in(key, 0)
    tensor_extent = (PARTITION_TOTAL, PARTITION_NODES, EMBED_BREADTH)
    result = jnp.clip(jax.random.normal(root_seed_handle, tensor_extent, jnp.float32), -5.0, 5.0)
    return result.astype(jnp.bfloat16)


def draw_proj_weights(key, part):
    key = jax.random.fold_in(key, 5)
    main_key = jax.random.fold_in(key, 0)
    spread = EMBED_BREADTH ** (-0.5)
    tensor_extent = (EMBED_BREADTH, 3, HEADS, HDIM)
    result = jnp.clip(jax.random.normal(main_key, tensor_extent, jnp.float32) * spread, -4.0 * spread, 4.0 * spread)
    return result.reshape(EMBED_BREADTH, 3, HEADS * HDIM).astype(jnp.bfloat16)


def block_scale(stream_key, dims, shards, least, top_value):
    def one(position, shards_of):
        draws = jax.random.uniform(jax.random.fold_in(jax.random.fold_in(stream_key, 6), position), (shards_of,), jnp.float32, least / len(shards), top_value / len(shards))
        return jnp.repeat(jnp.exp(draws), dims[position] // shards_of).reshape((-1,) + (1,) * (len(dims) - position - 1))

    gain = one(*shards[0])
    for cut in shards[1:]:
        gain = gain * one(*cut)
    return gain


def normal_values(key, extent, width, reach, cuts=(), kind=jnp.bfloat16):
    entries = jax.random.normal(key, extent, jnp.float32) * width
    if len(cuts) > 0:
        entries = block_scale(key, extent, cuts, -0.22, 0.18) * entries
    return jnp.clip(entries, min=-reach, max=reach).astype(kind)


def setup_inputs(seed: int = 0, part: int = 0) -> dict:
    keys = jax.random.split(jax.random.key(seed), 7)
    part_splits = jax.random.split(jax.random.fold_in(keys[6], part), 7)
    return {
        "node_features": draw_node_features(jax.random.fold_in(jax.random.fold_in(keys[6], part), 71), part),
        "result_cotangent": normal_values(part_splits[1], (PARTITION_TOTAL, PARTITION_NODES, ATTN_INNER_SIZE), 1.0, 6.0, ((0, 2), (1, 4), (2, 2))),
        "proj_weights": draw_proj_weights(jax.random.fold_in(keys[6], 71), part),
        "cluster_pairs": draw_cluster_pairs(jax.random.fold_in(jax.random.fold_in(keys[6], part), 71), part),
        "cluster_fill": draw_cluster_fill(jax.random.fold_in(jax.random.fold_in(keys[6], part), 71), part),
        "global_nodes": draw_global_nodes(jax.random.fold_in(jax.random.fold_in(keys[6], part), 71), part),
    }


NORM_EPS = 1e-06

def one_graph(graph_items, weights):
    features, cotangent, pair_list, fill_list, global_ids = graph_items
    score_scale = HDIM ** (-0.5)
    feats32 = features.astype(jnp.float32)
    inverse = lax.rsqrt(lax.optimization_barrier(jnp.mean(feats32 * feats32, -1, keepdims=True)) + NORM_EPS)
    normed32 = feats32 * inverse
    normed = normed32.astype(jnp.bfloat16)
    weights32 = weights.astype(jnp.float32)
    projected = jnp.einsum('nd,dif->nif', normed.astype(jnp.float32), weights32).astype(jnp.bfloat16)
    queries = projected[:, 0]
    keys_all = projected[:, 1]
    values_all = projected[:, 2]
    locations = jnp.arange(PARTITION_NODES, dtype=jnp.int32)
    real_node = locations % GROUP_VERTICES < fill_list[locations // GROUP_VERTICES]
    dout = jnp.where(real_node[:, None], cotangent, jnp.zeros_like(cotangent))
    cell_span = jnp.arange(GROUP_VERTICES, dtype=jnp.int32)

    def cluster_step(step_carry, cluster):
        key_acc, value_acc = step_carry
        start_row = cluster * GROUP_VERTICES
        query_block = lax.dynamic_slice_in_dim(queries, start_row, GROUP_VERTICES, 0)
        dout_block = lax.dynamic_slice_in_dim(dout, start_row, GROUP_VERTICES, 0)
        query_real = lax.dynamic_slice_in_dim(real_node, start_row, GROUP_VERTICES, 0)
        block_rows = (pair_list[cluster][:, None] * GROUP_VERTICES + cell_span[None, :]).reshape(-1).astype(jnp.int32)
        key_index = jnp.concatenate([block_rows, global_ids.astype(jnp.int32)])
        key_real = real_node[key_index]
        query_heads = query_block.astype(jnp.float32).reshape(GROUP_VERTICES, HEADS, HDIM)
        key_heads = keys_all[key_index].astype(jnp.float32).reshape(-1, HEADS, HDIM)
        value_heads = values_all[key_index].astype(jnp.float32).reshape(-1, HEADS, HDIM)
        dout_heads = dout_block.astype(jnp.float32).reshape(GROUP_VERTICES, HEADS, HDIM)
        scores = jnp.einsum('qhd,khd->hqk', query_heads, key_heads) * score_scale
        masked = jnp.where(key_real[None, None, :], scores, -1e+30)
        row_max = lax.optimization_barrier(jnp.max(masked, -1, keepdims=True))
        exp_terms = jnp.where(key_real[None, None, :], jnp.exp(masked - row_max), 0.0)
        attn_prob = exp_terms / lax.optimization_barrier(jnp.sum(exp_terms, -1, keepdims=True))
        prob_rounded = lax.optimization_barrier(attn_prob.astype(jnp.bfloat16)).astype(jnp.float32)
        output = jnp.einsum('hqk,khd->qhd', prob_rounded, value_heads).reshape(GROUP_VERTICES, ATTN_INNER_SIZE)
        output = jnp.where(query_real[:, None], output, 0.0).astype(jnp.bfloat16)
        dprob = jnp.einsum('qhd,khd->hqk', dout_heads, value_heads)
        row_delta = lax.optimization_barrier(jnp.sum(attn_prob * dprob, -1, keepdims=True))
        dscore = lax.optimization_barrier((attn_prob * (dprob - row_delta)).astype(jnp.bfloat16)).astype(jnp.float32)
        probe_derivative = (jnp.einsum('hqk,khd->qhd', dscore, key_heads) * score_scale).reshape(GROUP_VERTICES, ATTN_INNER_SIZE).astype(jnp.bfloat16)
        key_part = (jnp.einsum('hqk,qhd->khd', dscore, query_heads) * score_scale).reshape(-1, ATTN_INNER_SIZE)
        value_part = jnp.einsum('hqk,qhd->khd', prob_rounded, dout_heads).reshape(-1, ATTN_INNER_SIZE)
        key_acc = key_acc.at[key_index].add(key_part)
        value_acc = value_acc.at[key_index].add(value_part)
        return ((key_acc, value_acc), (output, probe_derivative))
    empty_starting_value = jnp.zeros((PARTITION_NODES, ATTN_INNER_SIZE), jnp.float32)
    (key_sum, value_sum), (results_list, probe_derivatives) = lax.scan(cluster_step, (empty_starting_value, empty_starting_value), jnp.arange(PARTITION_GROUPS, dtype=jnp.int32))
    mixed_result = results_list.reshape(PARTITION_NODES, ATTN_INNER_SIZE)
    probe_derivative = probe_derivatives.reshape(PARTITION_NODES, ATTN_INNER_SIZE)
    stacked = jnp.stack([probe_derivative, key_sum.astype(jnp.bfloat16), value_sum.astype(jnp.bfloat16)], 1)
    stacked32 = stacked.astype(jnp.float32)
    node_grad = jnp.einsum('nif,dif->nd', stacked32, weights32)
    grad_x = (inverse * (node_grad - normed32 * lax.optimization_barrier(jnp.mean(normed32 * node_grad, -1, keepdims=True)))).astype(jnp.bfloat16)
    grad_w = jnp.einsum('nd,nif->dif', normed.astype(jnp.float32), stacked32)
    return (mixed_result, grad_x, grad_w)

def reference(node_features, result_cotangent, proj_weights, cluster_pairs, cluster_fill, global_nodes):
    mixed_result, grad_x, grad_parts = lax.map(lambda graph_items: one_graph(graph_items, proj_weights), (node_features, result_cotangent, cluster_pairs, cluster_fill, global_nodes))
    return (mixed_result, grad_x, lax.optimization_barrier(jnp.sum(grad_parts, 0)))
```

```python
import functools

import jax
import jax.numpy as jnp
from jax import lax
from jax.experimental import pallas as pl
from jax.experimental.pallas import tpu as pltpu
from jax.sharding import PartitionSpec as P

HDIM = 64
GROUP_VERTICES = 128
PAIR = 2 * HDIM
NORM_EPS = 1e-06
LOG2E = 1.4426950408889634
F32 = jnp.float32
BF16 = jnp.bfloat16
VMEM_LIMIT = 48 * 1024 * 1024
NT = (((1,), (1,)), ((), ()))
NN = (((1,), (0,)), ((), ()))
TN = (((0,), (0,)), ((), ()))

VMEM = pl.BlockSpec(memory_space=pltpu.VMEM)
SMEM = pl.BlockSpec(memory_space=pltpu.SMEM)


def dot(a, b, dims=NN):
    return lax.dot_general(a, b, dims, preferred_element_type=F32)


def params():
    return pltpu.CompilerParams(vmem_limit_bytes=VMEM_LIMIT)


def project_kernel(shards, core_ref, ids_ref, w_ref, x_ref, *refs):
    near = refs[: shards - 1]
    far = refs[shards - 1 : 2 * (shards - 1)]
    normed_ref, q_ref, k_ref, v_ref = refs[2 * (shards - 1) :]
    nodes = x_ref.shape[0]
    rows = nodes // 2
    core = core_ref[0]

    def norm(block):
        wide = block.astype(F32)
        inverse = lax.rsqrt(jnp.mean(wide * wide, -1, keepdims=True) + NORM_EPS)
        return (wide * inverse).astype(BF16)

    def project(start, count):
        normed = normed_ref[pl.ds(start, count), :]
        q_ref[pl.ds(start, count), :] = dot(normed, w_ref[0]).astype(BF16)
        k_ref[pl.ds(start, count), :] = dot(normed, w_ref[1]).astype(BF16)
        v_ref[pl.ds(start, count), :] = dot(normed, w_ref[2]).astype(BF16)

    normed_ref[pl.ds(0, nodes), :] = norm(x_ref[...])
    project(0, nodes)
    for shard in range(1, shards):
        mine = pl.multiple_of(shard * nodes + core * rows, rows)
        other = pl.multiple_of(shard * nodes + (1 - core) * rows, rows)
        normed_ref[pl.ds(mine, rows), :] = norm(near[shard - 1][...])
        normed_ref[pl.ds(other, rows), :] = norm(far[shard - 1][...])
        project(shard * nodes, nodes)
    total = shards * nodes
    count = ids_ref.shape[0]
    key_sum = jnp.zeros((count, k_ref.shape[1]), F32)
    value_sum = key_sum
    for shard in range(shards):
        places = lax.broadcasted_iota(jnp.int32, (count, nodes), 1) + shard * nodes
        pick = jnp.where(places == ids_ref[...], 1.0, 0.0).astype(BF16)
        key_sum += dot(pick, k_ref[shard * nodes : (shard + 1) * nodes, :])
        value_sum += dot(pick, v_ref[shard * nodes : (shard + 1) * nodes, :])
    k_ref[total : total + count, :] = key_sum.astype(BF16)
    v_ref[total : total + count, :] = value_sum.astype(BF16)


def attend_kernel(shard, total, lookups, first, meta_ref, fill_ref, q_ref, dout_ref, k_ref, v_ref, *refs):
    if first:
        dq_ref, dk_ref, dv_ref, out_ref = refs
        dk_ref[...] = jnp.zeros_like(dk_ref)
        dv_ref[...] = jnp.zeros_like(dv_ref)
    else:
        dk_in, dv_in, dq_ref, dk_ref, dv_ref = refs
        dk_ref[...] = dk_in[...]
        dv_ref[...] = dv_in[...]
    size = GROUP_VERTICES
    clusters = dout_ref.shape[0] // size
    width = dout_ref.shape[1]
    count = k_ref.shape[0] - total
    lanes = lax.broadcasted_iota(jnp.int32, (size, PAIR), 1)
    low = lanes < HDIM
    rows = lax.broadcasted_iota(jnp.int32, (size, 1), 0)
    slots = lax.broadcasted_iota(jnp.int32, (size, 2 * size), 0)
    zero = jnp.zeros((), BF16)

    def split(block):
        return jnp.concatenate([jnp.where(low, block, zero), jnp.where(low, zero, block)], 0)

    @pl.loop(0, clusters)
    def _(cluster):
        base = (shard * clusters + cluster) * lookups
        starts = [pl.multiple_of(meta_ref[base + i] * size, size) for i in range(lookups)]
        fills = [fill_ref[base + i] for i in range(lookups)]
        place = pl.multiple_of(cluster * size, size)
        real = rows < fills[0]
        for column in range(0, width, PAIR):
            cols = slice(column, column + PAIR)
            queries = split(q_ref[pl.ds(shard * clusters * size + place, size), cols])
            douts = split(jnp.where(real, dout_ref[pl.ds(place, size), cols], zero))
            keys = jnp.concatenate(
                [k_ref[pl.ds(s, size), cols] for s in starts] + [k_ref[total:, cols]], 0
            )
            values = jnp.concatenate(
                [v_ref[pl.ds(s, size), cols] for s in starts] + [v_ref[total:, cols]], 0
            )
            scores = dot(keys, queries, NT)
            parts = [
                jnp.where(slots < fills[i], scores[i * size : (i + 1) * size], -1e30)
                for i in range(lookups)
            ]
            scores = jnp.concatenate(parts + [scores[lookups * size :]], 0)
            peak = jnp.max(scores, 0, keepdims=True)
            terms = jnp.exp2((scores - peak) * (LOG2E * HDIM ** (-0.5)))
            prob = terms * (1.0 / jnp.sum(terms, 0, keepdims=True))
            rounded = prob.astype(BF16)
            dprob = dot(values, douts, NT)
            delta = jnp.sum(prob * dprob, 0, keepdims=True)
            dscore = (prob * (dprob - delta)).astype(BF16)
            dv_part = dot(rounded, douts)
            dk_part = dot(dscore, queries) * HDIM ** (-0.5)
            for i in range(lookups):
                span = pl.ds(starts[i], size)
                dk_ref[span, cols] += dk_part[i * size : (i + 1) * size]
                dv_ref[span, cols] += dv_part[i * size : (i + 1) * size]
            dk_ref[total:, cols] += dk_part[lookups * size :]
            dv_ref[total:, cols] += dv_part[lookups * size :]
            dq = dot(keys, dscore, TN) * HDIM ** (-0.5)
            dq = jnp.concatenate([dq[:HDIM, :size], dq[HDIM:, size:]], 0)
            dq_ref[pl.ds(place, size), cols] = dq.T.astype(BF16)
            if first:
                mixed = dot(values, rounded, TN)
                mixed = jnp.concatenate([mixed[:HDIM, :size], mixed[HDIM:, size:]], 0)
                out_ref[pl.ds(place, size), cols] = jnp.where(real, mixed.T, 0.0).astype(BF16)


def finish_kernel(shards, reps, rep_ref, ids_ref, slices_ref, w_ref, dk_ref, dv_ref, *refs):
    dq_refs = refs[:shards]
    mine_ref, other_ref, node_ref = refs[shards:]
    nodes = dq_refs[0].shape[0]
    total = shards * nodes
    count = ids_ref.shape[1]
    share = mine_ref.shape[1]
    dkg, dvg = dk_ref[total:, :], dv_ref[total:, :]
    dkg_hi, dvg_hi = dkg.astype(BF16), dvg.astype(BF16)
    dkg_lo, dvg_lo = (dkg - dkg_hi.astype(F32)).astype(BF16), (dvg - dvg_hi.astype(F32)).astype(BF16)
    sums = [None, None, None]
    for shard in range(shards):
        span = slice(shard * nodes, (shard + 1) * nodes)
        places = lax.broadcasted_iota(jnp.int32, (nodes, count), 0) + shard * nodes
        put = jnp.where(places == ids_ref[...], 1.0, 0.0).astype(BF16)
        dk = (dk_ref[span, :] + (dot(put, dkg_hi) + dot(put, dkg_lo))).astype(BF16)
        dv = (dv_ref[span, :] + (dot(put, dvg_hi) + dot(put, dvg_lo))).astype(BF16)
        grads = [dq_refs[shard][...], dk, dv]
        left = slices_ref[:, span]
        for i in range(3):
            term = dot(left, grads[i])
            sums[i] = term if shard == 0 else sums[i] + term
        if shard == 0:
            node_ref[...] = dot(grads[0], w_ref[0], NT) + (
                dot(grads[1], w_ref[1], NT) + dot(grads[2], w_ref[2], NT)
            )
    for i in range(3):
        mine_ref[i] = sums[i][:share]
        other_ref[i] = sums[i][share:]


def local(node_features, result_cotangent, proj_weights, cluster_pairs, cluster_fill, global_nodes):
    features = node_features[0]
    cotangent = result_cotangent[0]
    pairs_here = cluster_pairs[0]
    fill_all = cluster_fill[0]
    global_ids = global_nodes[0]
    weights = jnp.transpose(proj_weights, (1, 0, 2))
    nodes, width = features.shape
    half_width = cotangent.shape[1]
    clusters, lookups = pairs_here.shape
    shards = lax.axis_size("seq")
    reps = lax.axis_size("rep")
    me = lax.axis_index("seq")
    core = lax.axis_index("tp")
    rep = lax.axis_index("rep")
    total = shards * nodes
    count = global_ids.shape[0]
    rows = nodes // 2

    def shift(value, step):
        return lax.ppermute(value, "seq", [(j, (j + step) % shards) for j in range(shards)])

    def swap(value, axis):
        return lax.ppermute(value, axis, [(0, 1), (1, 0)])

    half = lax.dynamic_slice_in_dim(features, core * rows, rows)
    near = [shift(half, step) for step in range(1, shards)]
    far = [swap(block, "tp") for block in near]
    pair_blocks = [pairs_here] + [shift(pairs_here, step) for step in range(1, shards)]
    anchor = near[-1]
    douts = [cotangent]
    for step in range(1, shards):
        ready, _ = lax.optimization_barrier((cotangent, anchor))
        douts.append(shift(ready, step))

    pairs = jnp.stack(pair_blocks).reshape(-1)
    meta = ((me - pairs // clusters) % shards) * clusters + pairs % clusters
    fills = jnp.sum(
        jnp.where(
            pairs[:, None] == jnp.arange(fill_all.shape[0], dtype=jnp.int32)[None], fill_all[None], 0
        ),
        -1,
    )
    ids = ((me - global_ids // nodes) % shards) * nodes + global_ids % nodes

    normed, q, k, v = pl.pallas_call(
        functools.partial(project_kernel, shards),
        out_shape=(
            jax.ShapeDtypeStruct((total, width), BF16),
            jax.ShapeDtypeStruct((total, half_width), BF16),
            jax.ShapeDtypeStruct((total + count, half_width), BF16),
            jax.ShapeDtypeStruct((total + count, half_width), BF16),
        ),
        in_specs=[SMEM] + [VMEM] * (3 + 2 * (shards - 1)),
        out_specs=(VMEM,) * 4,
        compiler_params=params(),
        name="project",
    )(core.reshape(1), ids[:, None], weights, features, *near, *far)

    share = width // (shards * reps)
    block = lax.dynamic_slice_in_dim(normed, me * reps * share, reps * share, 1).T
    block = jnp.roll(block, -rep * share, 0)

    dqs = []
    dk = dv = mixed = None
    acc = jax.ShapeDtypeStruct((total + count, half_width), F32)
    flat = jax.ShapeDtypeStruct((nodes, half_width), BF16)
    for shard in range(shards):
        first = shard == 0
        got = pl.pallas_call(
            functools.partial(attend_kernel, shard, total, lookups, first),
            out_shape=(flat, acc, acc) + ((flat,) if first else ()),
            in_specs=[SMEM, SMEM] + [VMEM] * (4 if first else 6),
            out_specs=(VMEM,) * (4 if first else 3),
            compiler_params=params(),
            name="attend_%d" % shard,
        )(meta, fills, q, douts[shard], k, v, *(() if first else (dk, dv)))
        dqs.append(got[0])
        dk, dv = got[1:3]
        if first:
            mixed = got[3]

    part = jax.ShapeDtypeStruct((3, share, half_width), F32)
    rest = jax.ShapeDtypeStruct((3, (reps - 1) * share, half_width), F32)
    mine, other, node_part = pl.pallas_call(
        functools.partial(finish_kernel, shards, reps),
        out_shape=(part, rest, jax.ShapeDtypeStruct((nodes, width), F32)),
        in_specs=[SMEM] + [VMEM] * (5 + shards),
        out_specs=(VMEM,) * 3,
        compiler_params=params(),
        name="finish",
    )(rep.reshape(1), ids[None, :], block, weights, dk, dv, *dqs)

    if reps == 2:
        grad_w = mine + swap(other, "rep")
    else:
        whole = jnp.roll(jnp.concatenate([mine, other], 1), rep * share, 1)
        grad_w = lax.psum_scatter(whole, "rep", scatter_dimension=1, tiled=True)
    node_grad = node_part + swap(node_part, "tp")
    wide = features.astype(F32)
    inverse = lax.rsqrt(jnp.mean(wide * wide, -1, keepdims=True) + NORM_EPS)
    normed32 = wide * inverse
    grad_x = inverse * (node_grad - normed32 * jnp.mean(normed32 * node_grad, -1, keepdims=True))
    return mixed[None], grad_x.astype(BF16)[None], jnp.transpose(grad_w, (1, 0, 2))


def solution(mesh):
    placed = (
        P(("groups", "rep"), "seq", None),
        P(("groups", "rep"), "seq", "tp"),
        P(None, None, "tp"),
        P(("groups", "rep"), "seq", None),
        P(("groups", "rep"), None),
        P(("groups", "rep"), None),
    )
    return jax.shard_map(
        local,
        mesh=mesh,
        in_specs=placed,
        out_specs=(
            P(("groups", "rep"), "seq", "tp"),
            P(("groups", "rep"), "seq", None),
            P(("groups", "seq", "rep"), None, "tp"),
        ),
        check_vma=False,
    )
```

```python
import functools

import jax
import jax.numpy as jnp
from jax import lax
from jax.experimental import pallas as pl
from jax.experimental.pallas import tpu as pltpu
from jax.sharding import PartitionSpec as P

HDIM = 64
GROUP_VERTICES = 128
PAIR = 2 * HDIM
TAIL = 16
CHUNK = 32
NORM_EPS = 1e-06
SCALE = HDIM ** (-0.5)
LOG2E = 1.4426950408889634
F32 = jnp.float32
BF16 = jnp.bfloat16
NT = (((1,), (1,)), ((), ()))
NN = (((1,), (0,)), ((), ()))
TN = (((0,), (0,)), ((), ()))

VMEM = pl.BlockSpec(memory_space=pltpu.VMEM)
SMEM = pl.BlockSpec(memory_space=pltpu.SMEM)
ANY = pl.BlockSpec(memory_space=pl.ANY)


def dot(a, b, dims=NN):
    return lax.dot_general(a, b, dims, preferred_element_type=F32)


def shape(dtype, *sizes):
    return jax.ShapeDtypeStruct(sizes, dtype)


def call(kernel, name, total, scalars, arrays, outs, scratch=(), micros=1, remote=()):
    spaces = [ANY if i in remote else VMEM for i in range(len(arrays))]
    return pl.pallas_call(
        kernel,
        out_shape=outs,
        in_specs=[SMEM] * len(scalars) + spaces,
        out_specs=(VMEM,) * len(outs),
        scratch_shapes=scratch,
        compiler_params=pltpu.CompilerParams(vmem_limit_bytes=(10 + 9 * total // 1024) << 20),
        cost_estimate=pl.CostEstimate(flops=micros * 10**9, bytes_accessed=0, transcendentals=0),
        name=name,
    )(*scalars, *arrays)


def prepare_kernel(place_ref, pairs_ref, x_ref, cotangent_ref, half_ref, dout_ref, sems):
    nodes, width = dout_ref.shape[0] - TAIL, dout_ref.shape[1]
    rows = half_ref.shape[0]
    start = pl.multiple_of(place_ref[1] * rows, rows)
    first = pltpu.make_async_copy(x_ref.at[pl.ds(start, rows), :], half_ref, sems.at[0])
    second = pltpu.make_async_copy(cotangent_ref, dout_ref.at[pl.ds(0, nodes), :], sems.at[1])
    first.start()
    second.start()
    lane = lax.broadcasted_iota(jnp.int32, (TAIL, width), 1)
    tail = jnp.zeros((TAIL, width), F32)
    clusters, lookups = pairs_ref.shape
    for index in range(clusters * lookups):
        entry = pairs_ref[index // lookups, index % lookups].astype(F32)
        tail = jnp.where(lane == index, entry, tail)
    dout_ref[nodes:, :] = tail.astype(BF16)
    first.wait()
    second.wait()


def norm(block):
    wide = block.astype(F32)
    inverse = lax.rsqrt(jnp.mean(wide * wide, -1, keepdims=True) + NORM_EPS)
    return (wide * inverse).astype(BF16)


def share_columns(place_ref, share, width):
    shift = place_ref[2] * place_ref[3]
    index = lax.broadcasted_iota(jnp.int32, (share, width), 0) + shift
    index = jnp.where(index >= share, index - share, index) + place_ref[0] * share
    columns = lax.broadcasted_iota(jnp.int32, (share, width), 1)
    return jnp.where(columns == index, 1.0, 0.0).astype(BF16)


def project_first_kernel(place_ref, row_ref, w_ref, x_ref, q_ref, k_ref, v_ref, left_ref, put_ref):
    normed = norm(x_ref[...])
    for i, ref in enumerate((q_ref, k_ref, v_ref)):
        ref[...] = dot(normed, w_ref[i]).astype(BF16)
    pick = share_columns(place_ref, left_ref.shape[0], normed.shape[1])
    left_ref[...] = dot(pick, normed, NT).astype(BF16)
    places = lax.broadcasted_iota(jnp.int32, put_ref.shape, 0)
    put_ref[...] = jnp.where(places == row_ref[...], 1.0, 0.0).astype(BF16)


def project_kernel(shards, place_ref, col_ref, w_ref, *refs):
    own, refs = refs[:4], refs[4:]
    near, refs = refs[: shards - 1], refs[shards - 1 :]
    far, refs = refs[: shards - 1], refs[shards - 1 :]
    q_ref, k_ref, v_ref, left_ref, normed_ref, sems = refs
    nodes = own[0].shape[0]
    rows = nodes // 2
    total = shards * nodes
    count = col_ref.shape[0]
    core = place_ref[1]
    copies = []
    for i, (ref, start) in enumerate(zip((q_ref, k_ref, v_ref), own)):
        copies.append(pltpu.make_async_copy(start, ref.at[pl.ds(0, nodes), :], sems.at[i]))
    copies.append(pltpu.make_async_copy(own[3], left_ref.at[:, pl.ds(0, nodes)], sems.at[3]))
    for copy in copies:
        copy.start()
    pick = share_columns(place_ref, left_ref.shape[0], normed_ref.shape[1])
    key_sum = jnp.zeros((count, k_ref.shape[1]), F32)
    value_sum = key_sum
    for shard in list(range(1, shards)) + [0]:
        span = slice(shard * nodes, (shard + 1) * nodes)
        if shard:
            mine = pl.multiple_of(core * rows, rows)
            other = pl.multiple_of((1 - core) * rows, rows)
            normed_ref[pl.ds(mine, rows), :] = norm(near[shard - 1][...])
            normed_ref[pl.ds(other, rows), :] = norm(far[shard - 1][...])
            normed = normed_ref[...]
            for i, ref in enumerate((q_ref, k_ref, v_ref)):
                ref[span, :] = dot(normed, w_ref[i]).astype(BF16)
            left_ref[:, span] = dot(pick, normed, NT).astype(BF16)
        else:
            for copy in copies:
                copy.wait()
        places = lax.broadcasted_iota(jnp.int32, (count, nodes), 1) + shard * nodes
        chosen = jnp.where(places == col_ref[...], 1.0, 0.0).astype(BF16)
        key_sum += dot(chosen, k_ref[span, :])
        value_sum += dot(chosen, v_ref[span, :])
    k_ref[total:, :] = key_sum.astype(BF16)
    v_ref[total:, :] = value_sum.astype(BF16)


def read_pairs(place_ref, fill_ref, dout_ref, nodes, clusters, lookups):
    tail = dout_ref[nodes:, :PAIR].astype(F32)
    lane = lax.broadcasted_iota(jnp.int32, tail.shape, 1)
    entries = []
    for index in range(clusters * lookups):
        cluster = jnp.max(jnp.where(lane == index, tail, 0.0)).astype(jnp.int32)
        block = (lax.div(cluster, clusters) ^ place_ref[0]) * clusters + lax.rem(cluster, clusters)
        entries.append((pl.multiple_of(block * GROUP_VERTICES, GROUP_VERTICES), fill_ref[cluster]))
    return [entries[i * lookups : (i + 1) * lookups] for i in range(clusters)]


def fold(block, op):
    result = block[:8]
    for start in range(8, block.shape[0], 8):
        result = op(result, block[start : start + 8])
    return result


def unit(slot, shard, total, entries, cluster, column, refs, accs, acc_cols, emit, scratch):
    q_ref, dout_ref, k_ref, v_ref = refs
    score_ref, dprob_ref, prob_ref, dscore_ref = (ref.at[slot] for ref in scratch)
    dk_ref, dv_ref = accs
    size = GROUP_VERTICES
    clusters = (dout_ref.shape[0] - TAIL) // size
    local_rows = len(entries) * size
    listed = local_rows + k_ref.shape[0] - total
    cols = slice(column, column + PAIR)
    state = {}
    places = [pl.ds(start, size) for start, _ in entries]
    places += [pl.ds(start, size) for start in range(total, k_ref.shape[0], size)]

    def split(block):
        low = lax.broadcasted_iota(jnp.int32, (size, PAIR), 1) < HDIM
        zero = jnp.zeros((), BF16)
        return jnp.concatenate([jnp.where(low, block, zero), jnp.where(low, zero, block)], 0)

    def load():
        start = (shard * clusters + cluster) * size
        real = lax.broadcasted_iota(jnp.int32, (size, 1), 0) < entries[0][1]
        douts = dout_ref[cluster * size : (cluster + 1) * size, cols]
        state["queries"] = split(q_ref[start : start + size, cols])
        state["douts"] = split(jnp.where(real, douts, jnp.zeros((), BF16)))

    def score_step(index):
        span = slice(index * size, (index + 1) * size)
        score_ref[span, :] = dot(k_ref[places[index], cols], state["queries"], NT)

    def dprob_step(index):
        span = slice(index * size, (index + 1) * size)
        dprob_ref[span, :] = dot(v_ref[places[index], cols], state["douts"], NT)

    def masked(start):
        block = score_ref[start : start + CHUNK, :]
        if start >= local_rows:
            return block
        slots = lax.broadcasted_iota(jnp.int32, (CHUNK, 2 * size), 0) + start % size
        return jnp.where(slots < entries[start // size][1], block, -1e30)

    def peak_step(start):
        part = fold(masked(start), jnp.maximum)
        state["peak"] = part if start == 0 else jnp.maximum(state["peak"], part)

    def term_step(start):
        if start == 0:
            state["peak"] = jnp.max(state["peak"], 0, keepdims=True)
        terms = jnp.exp2((masked(start) - state["peak"]) * (LOG2E * SCALE))
        weighted = fold(terms * dprob_ref[start : start + CHUNK, :], jnp.add)
        score_ref[start : start + CHUNK, :] = terms
        terms = fold(terms, jnp.add)
        state["sum"] = terms if start == 0 else state["sum"] + terms
        state["weighted"] = weighted if start == 0 else state["weighted"] + weighted

    def prob_step(start):
        if start == 0:
            state["inverse"] = 1.0 / jnp.sum(state["sum"], 0, keepdims=True)
            state["delta"] = jnp.sum(state["weighted"], 0, keepdims=True) * state["inverse"]
        span = slice(start, start + CHUNK)
        prob = score_ref[span, :] * state["inverse"]
        prob_ref[span, :] = prob.astype(BF16)
        dscore_ref[span, :] = (prob * (dprob_ref[span, :] - state["delta"])).astype(BF16)

    def value_step(index):
        span = slice(index * size, (index + 1) * size)
        dv_ref[places[index], acc_cols] += dot(prob_ref[span, :], state["douts"])

    def key_step(index):
        span = slice(index * size, (index + 1) * size)
        dk_ref[places[index], acc_cols] += dot(dscore_ref[span, :], state["queries"]) * SCALE

    def query_step():
        keys = jnp.concatenate([k_ref[place, cols] for place in places], 0)
        emit(cluster, column, joined(dot(keys, dscore_ref[...], TN) * SCALE).astype(BF16), prob_ref)

    step = functools.partial
    blocks, chunks = range(listed // size), range(0, listed, CHUNK)
    ahead = [load] + [step(f, i) for i in blocks for f in (score_step, dprob_step)]
    middle = [step(f, start) for f in (peak_step, term_step, prob_step) for start in chunks]
    behind = [step(f, i) for i in blocks for f in (value_step, key_step)] + [query_step]
    return ahead, middle, behind


def joined(block):
    size = GROUP_VERTICES
    return jnp.concatenate([block[:HDIM, :size], block[HDIM:, size:]], 0).T


def run_units(units):
    for step in units[0][0]:
        step()
    for index, (_, middle, _) in enumerate(units):
        beside = units[index - 1][2] if index else []
        beside = beside + (units[index + 1][0] if index + 1 < len(units) else [])
        done = 0
        for position, step in enumerate(middle):
            step()
            while done < (position + 1) * len(beside) // len(middle):
                beside[done]()
                done += 1
    for step in units[-1][2]:
        step()


def attend_kernel(shard, total, lookups, first, place_ref, fill_ref, q_ref, dout_ref, k_ref, v_ref, *refs):
    scratch, refs = refs[-4:], refs[:-4]
    if first:
        dq_ref, dk_ref, dv_ref, probs_ref = refs
        dk_ref[...] = jnp.zeros_like(dk_ref)
        dv_ref[...] = jnp.zeros_like(dv_ref)
    else:
        dk_in, dv_in, dq_ref, dk_ref, dv_ref = refs
        dk_ref[...] = dk_in[...]
        dv_ref[...] = dv_in[...]
    nodes, width = dq_ref.shape
    clusters = nodes // GROUP_VERTICES
    entries = read_pairs(place_ref, fill_ref, dout_ref, nodes, clusters, lookups)

    def emit(cluster, column, dq, prob_ref):
        dq_ref[cluster * GROUP_VERTICES : (cluster + 1) * GROUP_VERTICES, column : column + PAIR] = dq
        if first:
            probs_ref[cluster * (width // PAIR) + column // PAIR] = prob_ref[...]

    units = []
    for cluster in range(clusters):
        for column in range(0, width, PAIR):
            units.append(
                unit(
                    len(units) % 2, shard, total, entries[cluster], cluster, column,
                    (q_ref, dout_ref, k_ref, v_ref), (dk_ref, dv_ref),
                    slice(column, column + PAIR), emit, scratch,
                )
            )
    run_units(units)


def mix_kernel(total, lookups, place_ref, fill_ref, dout_ref, v_ref, probs_ref, out_ref):
    size = GROUP_VERTICES
    nodes, width = out_ref.shape
    clusters = nodes // size
    entries = read_pairs(place_ref, fill_ref, dout_ref, nodes, clusters, lookups)
    for cluster in range(clusters):
        real = lax.broadcasted_iota(jnp.int32, (size, 1), 0) < entries[cluster][0][1]
        for column in range(0, width, PAIR):
            cols = slice(column, column + PAIR)
            values = [v_ref[pl.ds(start, size), cols] for start, _ in entries[cluster]]
            values = jnp.concatenate(values + [v_ref[total:, cols]], 0)
            probs = probs_ref[cluster * (width // PAIR) + column // PAIR]
            mixed = jnp.where(real, joined(dot(values, probs, TN)), 0.0)
            out_ref[cluster * size : (cluster + 1) * size, cols] = mixed.astype(BF16)


def finish_kernel(shard, shards, total, lookups, column, place_ref, fill_ref, q_ref, dout_ref, k_ref, v_ref, *refs):
    scratch, refs = refs[-4:], refs[:-4]
    dk_in, dv_in, left_ref, put_ref = refs[:4]
    dq_refs, refs = refs[4 : 3 + shards], refs[3 + shards :]
    mine_ref, other_ref, own_ref, dk_ref, dv_ref, dq_ref = refs
    cols = slice(column, column + PAIR)
    dk_ref[...] = dk_in[:, cols]
    dv_ref[...] = dv_in[:, cols]
    nodes = dq_ref.shape[0]
    clusters = nodes // GROUP_VERTICES
    entries = read_pairs(place_ref, fill_ref, dout_ref, nodes, clusters, lookups)

    def emit(cluster, column, dq, prob_ref):
        dq_ref[cluster * GROUP_VERTICES : (cluster + 1) * GROUP_VERTICES, :] = dq

    run_units(
        [
            unit(
                cluster % 2, shard, total, entries[cluster], cluster, column,
                (q_ref, dout_ref, k_ref, v_ref), (dk_ref, dv_ref), slice(0, PAIR), emit, scratch,
            )
            for cluster in range(clusters)
        ]
    )
    share = mine_ref.shape[1]
    picked = []
    for ref in (dk_ref, dv_ref):
        wide = ref[total:, :]
        high = wide.astype(BF16)
        picked += [high, (wide - high.astype(F32)).astype(BF16)]
    picked = jnp.concatenate(picked, 1)
    sums = None
    order = iter(dq_refs)
    for block in range(shards):
        span = slice(block * nodes, (block + 1) * nodes)
        added = dot(put_ref[span, :], picked)
        dq = dq_ref[...] if block == shard else next(order)[:, cols]
        dk = (dk_ref[span, :] + (added[:, :PAIR] + added[:, PAIR : 2 * PAIR])).astype(BF16)
        dv = (dv_ref[span, :] + (added[:, 2 * PAIR : 3 * PAIR] + added[:, 3 * PAIR :])).astype(BF16)
        if block == 0:
            own_ref[0], own_ref[1], own_ref[2] = dq, dk, dv
        term = dot(left_ref[:, span], jnp.concatenate([dq, dk, dv], 1))
        sums = term if sums is None else sums + term
    for i in range(3):
        mine_ref[i] = sums[:share, i * PAIR : (i + 1) * PAIR]
        other_ref[i] = sums[share:, i * PAIR : (i + 1) * PAIR]


def node_kernel(w_ref, *refs):
    node_ref = refs[-1]
    total = None
    for i in range(3):
        grads = jnp.concatenate([ref[i] for ref in refs[:-1]], 1)
        part = dot(grads, w_ref[i], NT)
        total = part if total is None else total + part
    node_ref[...] = total


def join_kernel(*refs):
    out_ref = refs[-1]
    half = (len(refs) - 1) // 2
    for index in range(half):
        cols = slice(index * PAIR, (index + 1) * PAIR)
        out_ref[:, :, cols] = refs[index][...] + refs[half + index][...]


def local(node_features, result_cotangent, proj_weights, cluster_pairs, cluster_fill, global_nodes):
    features = node_features[0]
    cotangent = result_cotangent[0]
    pairs = cluster_pairs[0]
    fill = cluster_fill[0]
    global_ids = global_nodes[0]
    weights = jnp.transpose(proj_weights, (1, 0, 2))
    nodes, width = features.shape
    half_width = cotangent.shape[1]
    lookups = pairs.shape[1]
    shards = lax.axis_size("seq")
    reps = lax.axis_size("rep")
    me = lax.axis_index("seq")
    total = shards * nodes
    count = global_ids.shape[0]
    share = width // (shards * reps)
    place = jnp.stack([me, lax.axis_index("tp"), lax.axis_index("rep"), jnp.int32(share)])
    place = place.astype(jnp.int32)

    def trade(value, step):
        return lax.ppermute(value, "seq", [(j, j ^ step) for j in range(shards)])

    def swap(value, axis):
        return lax.ppermute(value, axis, [(0, 1), (1, 0)])

    half, dout = call(
        prepare_kernel, "prepare", total, (place, pairs), (features, cotangent),
        (shape(BF16, nodes // 2, width), shape(BF16, nodes + TAIL, half_width)),
        (pltpu.SemaphoreType.DMA((2,)),), remote=(0, 1),
    )
    steps = [1] + list(range(shards - 1, 1, -1))
    near = {step: trade(half, step) for step in steps}
    far = {step: swap(near[step], "tp") for step in steps}
    douts = {0: dout}
    for step in steps:
        ready, _ = lax.optimization_barrier((dout, near[step]))
        douts[step] = trade(ready, step)

    ids = ((global_ids // nodes) ^ me) * nodes + global_ids % nodes
    flat = shape(BF16, nodes, half_width)
    *own, put = call(
        project_first_kernel, "project_first", total, (place,), (ids[None, :], weights, features),
        (flat, flat, flat, shape(BF16, reps * share, nodes), shape(BF16, total, count)),
    )
    others = range(1, shards)
    q, k, v, left = call(
        functools.partial(project_kernel, shards), "project", total, (place,),
        (ids[:, None], weights, *own, *[near[i] for i in others], *[far[i] for i in others]),
        (
            shape(BF16, total, half_width),
            shape(BF16, total + count, half_width),
            shape(BF16, total + count, half_width),
            shape(BF16, reps * share, total),
        ),
        (pltpu.VMEM((nodes, width), BF16), pltpu.SemaphoreType.DMA((4,))),
        micros=4, remote=(2, 3, 4, 5),
    )

    acc = shape(F32, total + count, half_width)
    listed = lookups * GROUP_VERTICES + count
    grid = (listed, 2 * GROUP_VERTICES)
    probs = shape(BF16, nodes // GROUP_VERTICES * (half_width // PAIR), *grid)
    scratch = tuple(pltpu.VMEM((2,) + grid, kind) for kind in (F32, F32, BF16, BF16))
    dqs = {}
    dk = dv = kept = None
    for shard in [0] + steps[:-1]:
        first = shard == 0
        got = call(
            functools.partial(attend_kernel, shard, total, lookups, first), "attend_%d" % shard, total,
            (place, fill), (q, douts[shard], k, v) + (() if first else (dk, dv)),
            (flat, acc, acc) + ((probs,) if first else ()), scratch, micros=4,
        )
        dqs[shard], dk, dv = got[:3]
        if first:
            kept = got[3]
    last = steps[-1]
    mine, other, grads = [], [], []
    for column in range(0, half_width, PAIR):
        got = call(
            functools.partial(finish_kernel, last, shards, total, lookups, column),
            "finish_%d" % column, total, (place, fill),
            (q, douts[last], k, v, dk, dv, left, put) + tuple(dqs[i] for i in sorted(dqs)),
            (
                shape(F32, 3, share, PAIR),
                shape(F32, 3, (reps - 1) * share, PAIR),
                shape(BF16, 3, nodes, PAIR),
            ),
            (
                pltpu.VMEM((total + count, PAIR), F32),
                pltpu.VMEM((total + count, PAIR), F32),
                pltpu.VMEM((nodes, PAIR), BF16),
            ) + scratch,
            micros=3,
        )
        mine.append(got[0])
        other.append(got[1])
        grads.append(got[2])
    node_part = call(node_kernel, "node", total, (), (weights, *grads), (shape(F32, nodes, width),))[0]
    later, _ = lax.optimization_barrier((kept, node_part))
    mixed = call(
        functools.partial(mix_kernel, total, lookups), "mix", total, (place, fill), (dout, v, later), (flat,)
    )[0]

    if reps == 2:
        back = [swap(block, "rep") for block in other]
        grad_w = call(join_kernel, "join", total, (), (*mine, *back), (shape(F32, 3, share, half_width),))[0]
    else:
        whole = jnp.concatenate([jnp.concatenate(mine, 2), jnp.concatenate(other, 2)], 1)
        whole = jnp.roll(whole, place[2] * share, 1)
        grad_w = lax.psum_scatter(whole, "rep", scatter_dimension=1, tiled=True)
    node_grad = node_part + swap(node_part, "tp")
    wide = features.astype(F32)
    inverse = lax.rsqrt(jnp.mean(wide * wide, -1, keepdims=True) + NORM_EPS)
    normed32 = wide * inverse
    grad_x = inverse * (node_grad - normed32 * jnp.mean(normed32 * node_grad, -1, keepdims=True))
    return mixed[None], grad_x.astype(BF16)[None], jnp.transpose(grad_w, (1, 0, 2))


def solution(mesh):
    placed = (
        P(("groups", "rep"), "seq", None),
        P(("groups", "rep"), "seq", "tp"),
        P(None, None, "tp"),
        P(("groups", "rep"), "seq", None),
        P(("groups", "rep"), None),
        P(("groups", "rep"), None),
    )
    return jax.shard_map(
        local,
        mesh=mesh,
        in_specs=placed,
        out_specs=(
            P(("groups", "rep"), "seq", "tp"),
            P(("groups", "rep"), "seq", None),
            P(("groups", "seq", "rep"), None, "tp"),
        ),
        check_vma=False,
    )
```

```python
import functools

import jax
import jax.numpy as jnp
from jax import lax
from jax.experimental import pallas as pl
from jax.experimental.pallas import tpu as pltpu
from jax.sharding import PartitionSpec as P

HDIM = 64
GROUP_VERTICES = 128
PAIR = 2 * HDIM
TAIL = 16
CHUNK = 32
BATCH = 4
NORM_EPS = 1e-06
SCALE = HDIM ** (-0.5)
LOG2E = 1.4426950408889634
F32 = jnp.float32
BF16 = jnp.bfloat16
NT = (((1,), (1,)), ((), ()))
NN = (((1,), (0,)), ((), ()))
TN = (((0,), (0,)), ((), ()))

VMEM = pl.BlockSpec(memory_space=pltpu.VMEM)
SMEM = pl.BlockSpec(memory_space=pltpu.SMEM)


def dot(a, b, dims=NN):
    return lax.dot_general(a, b, dims, preferred_element_type=F32)


def shape(dtype, *sizes):
    return jax.ShapeDtypeStruct(sizes, dtype)


def call(kernel, name, total, scalars, arrays, outs, scratch=(), micros=0):
    return pl.pallas_call(
        kernel,
        out_shape=outs,
        in_specs=[SMEM] * len(scalars) + [VMEM] * len(arrays),
        out_specs=(VMEM,) * len(outs),
        scratch_shapes=scratch,
        compiler_params=pltpu.CompilerParams(vmem_limit_bytes=(10 + 9 * total // 1024) << 20),
        cost_estimate=pl.CostEstimate(flops=micros * 10**9, bytes_accessed=0, transcendentals=0),
        name=name,
    )(*scalars, *arrays)


def prepare_kernel(pairs_ref, cotangent_ref, dout_ref):
    nodes, width = cotangent_ref.shape
    dout_ref[:nodes, :] = cotangent_ref[...]
    row = lax.broadcasted_iota(jnp.int32, (TAIL, width), 0)
    lane = lax.broadcasted_iota(jnp.int32, (TAIL, width), 1)
    tail = jnp.zeros((TAIL, width), F32)
    clusters, lookups = pairs_ref.shape
    for index in range(clusters * lookups):
        entry = pairs_ref[index // lookups, index % lookups].astype(F32)
        tail = jnp.where((row == 0) & (lane == index), entry, tail)
    dout_ref[nodes:, :] = tail.astype(BF16)


def norm(block):
    wide = block.astype(F32)
    inverse = lax.rsqrt(jnp.mean(wide * wide, -1, keepdims=True) + NORM_EPS)
    return (wide * inverse).astype(BF16)


def share_columns(share, width):
    shift = lax.axis_index("rep") * (share // lax.axis_size("rep"))
    index = lax.broadcasted_iota(jnp.int32, (share, width), 0) + shift
    index = jnp.where(index >= share, index - share, index) + lax.axis_index("seq") * share
    columns = lax.broadcasted_iota(jnp.int32, (share, width), 1)
    return jnp.where(columns == index, 1.0, 0.0).astype(BF16)


def project_first_kernel(row_ref, col_ref, w_ref, x_ref, q_ref, k_ref, v_ref, left_ref, put_ref, pick_ref):
    normed = norm(x_ref[...])
    for i, ref in enumerate((q_ref, k_ref, v_ref)):
        ref[...] = dot(normed, w_ref[i]).astype(BF16)
    left_ref[...] = dot(share_columns(*left_ref.shape[:1], normed.shape[1]), normed, NT).astype(BF16)
    places = lax.broadcasted_iota(jnp.int32, put_ref.shape, 0)
    put_ref[...] = jnp.where(places == row_ref[...], 1.0, 0.0).astype(BF16)
    places = lax.broadcasted_iota(jnp.int32, pick_ref.shape, 1)
    pick_ref[...] = jnp.where(places == col_ref[...], 1.0, 0.0).astype(BF16)


def project_next_kernel(w_ref, near_ref, far_ref, q_ref, k_ref, v_ref, left_ref, normed_ref):
    rows = near_ref.shape[0]
    core = lax.axis_index("tp")
    normed_ref[pl.ds(pl.multiple_of(core * rows, rows), rows), :] = norm(near_ref[...])
    normed_ref[pl.ds(pl.multiple_of((1 - core) * rows, rows), rows), :] = norm(far_ref[...])
    normed = normed_ref[...]
    for i, ref in enumerate((q_ref, k_ref, v_ref)):
        ref[...] = dot(normed, w_ref[i]).astype(BF16)
    left_ref[...] = dot(share_columns(*left_ref.shape[:1], normed.shape[1]), normed, NT).astype(BF16)


def project_kernel(shards, w_ref, pick_ref, *refs):
    early, refs = refs[:8], refs[8:]
    near, refs = refs[: shards - 2], refs[shards - 2 :]
    far, refs = refs[: shards - 2], refs[shards - 2 :]
    q_ref, k_ref, v_ref, left_ref, normed_ref = refs
    nodes = early[0].shape[0]
    rows = nodes // 2
    total = shards * nodes
    core = lax.axis_index("tp")
    for i, early_ref in enumerate(early):
        span = slice(i // 4 * nodes, (i // 4 + 1) * nodes)
        if i % 4 == 3:
            left_ref[:, span] = early_ref[...]
        else:
            (q_ref, k_ref, v_ref)[i % 4][span, :] = early_ref[...]
    for shard in range(2, shards):
        mine = pl.multiple_of((shard - 2) * nodes + core * rows, rows)
        other = pl.multiple_of((shard - 2) * nodes + (1 - core) * rows, rows)
        normed_ref[pl.ds(mine, rows), :] = norm(near[shard - 2][...])
        normed_ref[pl.ds(other, rows), :] = norm(far[shard - 2][...])
    columns = share_columns(left_ref.shape[0], normed_ref.shape[1])
    for start in range(2 * nodes, total, BATCH * nodes):
        stop = min(start + BATCH * nodes, total)
        normed = normed_ref[start - 2 * nodes : stop - 2 * nodes, :]
        for i, ref in enumerate((q_ref, k_ref, v_ref)):
            ref[start:stop, :] = dot(normed, w_ref[i]).astype(BF16)
        left_ref[:, start:stop] = dot(columns, normed, NT).astype(BF16)
    key_sum = value_sum = None
    for start in range(0, total, BATCH * nodes):
        stop = min(start + BATCH * nodes, total)
        pick = pick_ref[:, start:stop]
        keys, values = dot(pick, k_ref[start:stop, :]), dot(pick, v_ref[start:stop, :])
        key_sum = keys if start == 0 else key_sum + keys
        value_sum = values if start == 0 else value_sum + values
    k_ref[total:, :] = key_sum.astype(BF16)
    v_ref[total:, :] = value_sum.astype(BF16)


def read_pairs(fill_ref, dout_ref, nodes, clusters, lookups):
    tail = dout_ref[nodes:, :PAIR].astype(F32)
    lane = lax.broadcasted_iota(jnp.int32, tail.shape, 1)
    base = fill_ref.shape[0]
    weight = jnp.zeros(tail.shape, F32)
    for index in range(clusters * lookups):
        weight = jnp.where(lane == index, float(base**index), weight)
    code = jnp.sum(tail * weight).astype(jnp.int32)
    me = lax.axis_index("seq")
    entries = []
    for index in range(clusters * lookups):
        cluster = lax.rem(lax.div(code, base**index), base)
        block = (lax.div(cluster, clusters) ^ me) * clusters + lax.rem(cluster, clusters)
        entries.append((pl.multiple_of(block * GROUP_VERTICES, GROUP_VERTICES), fill_ref[cluster]))
    return [entries[i * lookups : (i + 1) * lookups] for i in range(clusters)]


def fold(block, op):
    result = block[:8]
    for start in range(8, block.shape[0], 8):
        result = op(result, block[start : start + 8])
    return result


def unit(slot, shard, total, entries, cluster, column, refs, accs, acc_cols, emit, scratch):
    q_ref, dout_ref, k_ref, v_ref = refs
    score_ref, dprob_ref, prob_ref, dscore_ref = (ref.at[slot] for ref in scratch)
    dk_ref, dv_ref = accs
    size = GROUP_VERTICES
    clusters = (dout_ref.shape[0] - TAIL) // size
    local_rows = len(entries) * size
    listed = local_rows + k_ref.shape[0] - total
    cols = slice(column, column + PAIR)
    state = {}
    places = [pl.ds(start, size) for start, _ in entries]
    places += [pl.ds(start, size) for start in range(total, k_ref.shape[0], size)]

    def split(block):
        low = lax.broadcasted_iota(jnp.int32, (size, PAIR), 1) < HDIM
        zero = jnp.zeros((), BF16)
        return jnp.concatenate([jnp.where(low, block, zero), jnp.where(low, zero, block)], 0)

    def load():
        start = (shard * clusters + cluster) * size
        real = lax.broadcasted_iota(jnp.int32, (size, 1), 0) < entries[0][1]
        douts = dout_ref[cluster * size : (cluster + 1) * size, cols]
        state["queries"] = split(q_ref[start : start + size, cols])
        state["douts"] = split(jnp.where(real, douts, jnp.zeros((), BF16)))

    def score_step(index):
        span = slice(index * size, (index + 1) * size)
        score_ref[span, :] = dot(k_ref[places[index], cols], state["queries"], NT)

    def dprob_step(index):
        span = slice(index * size, (index + 1) * size)
        dprob_ref[span, :] = dot(v_ref[places[index], cols], state["douts"], NT)

    def masked(start):
        block = score_ref[start : start + CHUNK, :]
        if start >= local_rows:
            return block
        slots = lax.broadcasted_iota(jnp.int32, (CHUNK, 2 * size), 0) + start % size
        return jnp.where(slots < entries[start // size][1], block, -1e30)

    def peak_step(start):
        part = fold(masked(start), jnp.maximum)
        state["peak"] = part if start == 0 else jnp.maximum(state["peak"], part)

    def term_step(start):
        if start == 0:
            state["peak"] = jnp.max(state["peak"], 0, keepdims=True)
        terms = jnp.exp2((masked(start) - state["peak"]) * (LOG2E * SCALE))
        weighted = fold(terms * dprob_ref[start : start + CHUNK, :], jnp.add)
        score_ref[start : start + CHUNK, :] = terms
        terms = fold(terms, jnp.add)
        state["sum"] = terms if start == 0 else state["sum"] + terms
        state["weighted"] = weighted if start == 0 else state["weighted"] + weighted

    def prob_step(start):
        if start == 0:
            state["inverse"] = 1.0 / jnp.sum(state["sum"], 0, keepdims=True)
            state["delta"] = jnp.sum(state["weighted"], 0, keepdims=True) * state["inverse"]
        span = slice(start, start + CHUNK)
        prob = score_ref[span, :] * state["inverse"]
        prob_ref[span, :] = prob.astype(BF16)
        dscore_ref[span, :] = (prob * (dprob_ref[span, :] - state["delta"])).astype(BF16)

    def value_step(index):
        span = slice(index * size, (index + 1) * size)
        dv_ref[places[index], acc_cols] += dot(prob_ref[span, :], state["douts"])

    def key_step(index):
        span = slice(index * size, (index + 1) * size)
        dk_ref[places[index], acc_cols] += dot(dscore_ref[span, :], state["queries"]) * SCALE

    def query_step():
        keys = jnp.concatenate([k_ref[place, cols] for place in places], 0)
        emit(cluster, column, joined(dot(keys, dscore_ref[...], TN) * SCALE).astype(BF16), prob_ref)

    step = functools.partial
    blocks, chunks = range(listed // size), range(0, listed, CHUNK)
    ahead = [load] + [step(f, i) for i in blocks for f in (score_step, dprob_step)]
    middle = [step(f, start) for f in (peak_step, term_step, prob_step) for start in chunks]
    behind = [step(f, i) for i in blocks for f in (value_step, key_step)] + [query_step]
    return ahead, middle, behind


def joined(block):
    size = GROUP_VERTICES
    return jnp.concatenate([block[:HDIM, :size], block[HDIM:, size:]], 0).T


def run_units(units):
    for step in units[0][0]:
        step()
    for index, (_, middle, _) in enumerate(units):
        beside = units[index - 1][2] if index else []
        beside = beside + (units[index + 1][0] if index + 1 < len(units) else [])
        done = 0
        for position, step in enumerate(middle):
            step()
            while done < (position + 1) * len(beside) // len(middle):
                beside[done]()
                done += 1
    for step in units[-1][2]:
        step()


def attend_kernel(group, total, lookups, first, fill_ref, q_ref, k_ref, v_ref, *refs):
    scratch, refs = refs[-4:], refs[:-4]
    dout_refs, refs = refs[: len(group)], refs[len(group) :]
    if first:
        dk_ref, dv_ref, probs_ref, *dq_refs = refs
        dk_ref[...] = jnp.zeros_like(dk_ref)
        dv_ref[...] = jnp.zeros_like(dv_ref)
    else:
        dk_in, dv_in, dk_ref, dv_ref, *dq_refs = refs
        dk_ref[...] = dk_in[...]
        dv_ref[...] = dv_in[...]
    nodes, width = dq_refs[0].shape
    clusters = nodes // GROUP_VERTICES

    def emit_to(shard, dq_ref):
        def emit(cluster, column, dq, prob_ref):
            dq_ref[cluster * GROUP_VERTICES : (cluster + 1) * GROUP_VERTICES, column : column + PAIR] = dq
            if shard == 0:
                probs_ref[cluster * (width // PAIR) + column // PAIR] = prob_ref[...]

        return emit

    units = []
    for shard, dout_ref, dq_ref in zip(group, dout_refs, dq_refs):
        entries = read_pairs(fill_ref, dout_ref, nodes, clusters, lookups)
        for cluster in range(clusters):
            for column in range(0, width, PAIR):
                units.append(
                    unit(
                        len(units) % 2, shard, total, entries[cluster], cluster, column,
                        (q_ref, dout_ref, k_ref, v_ref), (dk_ref, dv_ref),
                        slice(column, column + PAIR), emit_to(shard, dq_ref), scratch,
                    )
                )
    run_units(units)


def mix_kernel(total, lookups, fill_ref, dout_ref, v_ref, probs_ref, out_ref):
    size = GROUP_VERTICES
    nodes, width = out_ref.shape
    clusters = nodes // size
    entries = read_pairs(fill_ref, dout_ref, nodes, clusters, lookups)
    for cluster in range(clusters):
        real = lax.broadcasted_iota(jnp.int32, (size, 1), 0) < entries[cluster][0][1]
        for column in range(0, width, PAIR):
            cols = slice(column, column + PAIR)
            values = [v_ref[pl.ds(start, size), cols] for start, _ in entries[cluster]]
            values = jnp.concatenate(values + [v_ref[total:, cols]], 0)
            probs = probs_ref[cluster * (width // PAIR) + column // PAIR]
            mixed = jnp.where(real, joined(dot(values, probs, TN)), 0.0)
            out_ref[cluster * size : (cluster + 1) * size, cols] = mixed.astype(BF16)


def finish_kernel(shard, shards, total, lookups, column, final, fill_ref, q_ref, dout_ref, k_ref, v_ref, *refs):
    scratch, refs = refs[-4:], refs[:-4]
    dk_in, dv_in, left_ref, put_ref = refs[:4]
    dq_refs, refs = refs[4 : 3 + shards], refs[3 + shards :]
    own_refs = []
    if final:
        w_ref, own_refs, refs = refs[0], list(refs[1 : 1 + column // PAIR]), refs[1 + column // PAIR :]
    mine_ref, other_ref, own_ref, dk_ref, dv_ref, dq_ref, all_ref = refs
    cols = slice(column, column + PAIR)
    dk_ref[...] = dk_in[:, cols]
    dv_ref[...] = dv_in[:, cols]
    nodes = dq_ref.shape[0]
    clusters = nodes // GROUP_VERTICES
    entries = read_pairs(fill_ref, dout_ref, nodes, clusters, lookups)

    def emit(cluster, column, dq, prob_ref):
        dq_ref[cluster * GROUP_VERTICES : (cluster + 1) * GROUP_VERTICES, :] = dq

    run_units(
        [
            unit(
                cluster % 2, shard, total, entries[cluster], cluster, column,
                (q_ref, dout_ref, k_ref, v_ref), (dk_ref, dv_ref), slice(0, PAIR), emit, scratch,
            )
            for cluster in range(clusters)
        ]
    )
    share = mine_ref.shape[1]
    wide = jnp.concatenate([dk_ref[total:, :], dv_ref[total:, :]], 1)
    high = wide.astype(BF16)
    picked = jnp.concatenate([high, (wide - high.astype(F32)).astype(BF16)], 0)
    order = iter(dq_refs)
    for block in range(shards):
        span = slice(block * nodes, (block + 1) * nodes)
        put = put_ref[span, :]
        added = dot(jnp.concatenate([put, put], 1), picked)
        all_ref[span, :PAIR] = dq_ref[...] if block == shard else next(order)[:, cols]
        all_ref[span, PAIR : 2 * PAIR] = (dk_ref[span, :] + added[:, :PAIR]).astype(BF16)
        all_ref[span, 2 * PAIR :] = (dv_ref[span, :] + added[:, PAIR:]).astype(BF16)
    sums = None
    for start in range(0, total, BATCH * nodes):
        stop = min(start + BATCH * nodes, total)
        term = dot(left_ref[:, start:stop], all_ref[start:stop, :])
        sums = term if start == 0 else sums + term
    for i in range(3):
        mine_ref[i] = sums[:share, i * PAIR : (i + 1) * PAIR]
        other_ref[i] = sums[share:, i * PAIR : (i + 1) * PAIR]
    if not final:
        own_ref[...] = all_ref[:nodes, :]
        return
    node = None
    for i in range(3):
        part = slice(i * PAIR, (i + 1) * PAIR)
        grads = [ref[:, part] for ref in own_refs] + [all_ref[:nodes, part]]
        term = dot(jnp.concatenate(grads, 1), w_ref[i], NT)
        node = term if node is None else node + term
    own_ref[...] = node


def features_kernel(x_ref, mine_ref, other_ref, out_ref):
    wide = x_ref[...].astype(F32)
    inverse = lax.rsqrt(jnp.mean(wide * wide, -1, keepdims=True) + NORM_EPS)
    normed = wide * inverse
    grad = mine_ref[...] + other_ref[...]
    out_ref[...] = (inverse * (grad - normed * jnp.mean(normed * grad, -1, keepdims=True))).astype(BF16)


def join_kernel(*refs):
    out_ref = refs[-1]
    half = (len(refs) - 1) // 2
    for index in range(half):
        cols = slice(index * PAIR, (index + 1) * PAIR)
        out_ref[:, :, cols] = refs[index][...] + refs[half + index][...]


def local(node_features, result_cotangent, proj_weights, cluster_pairs, cluster_fill, global_nodes):
    features = node_features[0]
    cotangent = result_cotangent[0]
    pairs = cluster_pairs[0]
    fill = cluster_fill[0]
    global_ids = global_nodes[0]
    weights = jnp.transpose(proj_weights, (1, 0, 2))
    nodes, width = features.shape
    half_width = cotangent.shape[1]
    lookups = pairs.shape[1]
    shards = lax.axis_size("seq")
    reps = lax.axis_size("rep")
    me = lax.axis_index("seq")
    total = shards * nodes
    count = global_ids.shape[0]
    share = width // (shards * reps)

    def trade(value, step):
        return lax.ppermute(value, "seq", [(j, j ^ step) for j in range(shards)])

    def swap(value, axis):
        return lax.ppermute(value, axis, [(0, 1), (1, 0)])

    half = lax.dynamic_slice_in_dim(features, lax.axis_index("tp") * (nodes // 2), nodes // 2)
    steps = list(range(1, shards))
    near = {step: trade(half, step) for step in steps}
    far = {1: swap(near[1], "tp")}
    ready, _ = lax.optimization_barrier((cotangent, near[1]))
    dout = call(
        prepare_kernel, "prepare", total, (pairs,), (ready,), (shape(BF16, nodes + TAIL, half_width),),
        micros=1,
    )[0]
    douts = {0: dout, 1: trade(dout, 1)}
    ids = ((global_ids // nodes) ^ me) * nodes + global_ids % nodes
    flat = shape(BF16, nodes, half_width)
    columns = shape(BF16, reps * share, nodes)
    *first, put, pick = call(
        project_first_kernel, "project_first", total, (),
        (ids[None, :], ids[:, None], weights, features),
        (flat, flat, flat, columns, shape(BF16, total, count), shape(BF16, count, total)), micros=2,
    )
    second = call(
        project_next_kernel, "project_next", total, (), (weights, near[1], far[1]),
        (flat, flat, flat, columns), (pltpu.VMEM((nodes, width), BF16),), micros=2,
    )
    for step in steps[1:]:
        near[step], _ = lax.optimization_barrier((near[step], (first[0], second[0])))
        far[step] = swap(near[step], "tp")
    ready, _ = lax.optimization_barrier((dout, [near[step] for step in steps]))
    for step in steps[1:]:
        douts[step] = trade(ready, step)
    q, k, v, left = call(
        functools.partial(project_kernel, shards), "project", total, (),
        (weights, pick, *first, *second, *[near[i] for i in steps[1:]], *[far[i] for i in steps[1:]]),
        (
            shape(BF16, total, half_width),
            shape(BF16, total + count, half_width),
            shape(BF16, total + count, half_width),
            shape(BF16, reps * share, total),
        ),
        (pltpu.VMEM((total - 2 * nodes, width), BF16),),
    )

    acc = shape(F32, total + count, half_width)
    listed = lookups * GROUP_VERTICES + count
    grid = (listed, 2 * GROUP_VERTICES)
    probs = shape(BF16, nodes // GROUP_VERTICES * (half_width // PAIR), *grid)
    scratch = tuple(pltpu.VMEM((2,) + grid, kind) for kind in (F32, F32, BF16, BF16))
    dqs = {}
    dk = dv = kept = None
    for group in [[0] + steps[:1]] + [[step] for step in steps[1:-1]]:
        first = 0 in group
        got = call(
            functools.partial(attend_kernel, group, total, lookups, first), "attend_%d" % group[-1], total,
            (fill,), (q, k, v, *[douts[i] for i in group]) + (() if first else (dk, dv)),
            (acc, acc) + ((probs,) if first else ()) + (flat,) * len(group), scratch,
        )
        dk, dv = got[:2]
        kept = got[2] if first else kept
        dqs.update(zip(group, got[-len(group) :]))
    last = steps[-1]
    mine, other, grads = [], [], []
    for column in range(0, half_width, PAIR):
        final = column + PAIR == half_width
        got = call(
            functools.partial(finish_kernel, last, shards, total, lookups, column, final),
            "finish_%d" % column, total, (fill,),
            (q, douts[last], k, v, dk, dv, left, put)
            + tuple(dqs[i] for i in sorted(dqs)) + ((weights, *grads) if final else ()),
            (
                shape(F32, 3, share, PAIR),
                shape(F32, 3, (reps - 1) * share, PAIR),
                shape(F32, nodes, width) if final else shape(BF16, nodes, 3 * PAIR),
            ),
            (
                pltpu.VMEM((total + count, PAIR), F32),
                pltpu.VMEM((total + count, PAIR), F32),
                pltpu.VMEM((nodes, PAIR), BF16),
                pltpu.VMEM((total, 3 * PAIR), BF16),
            ) + scratch,
        )
        mine.append(got[0])
        other.append(got[1])
        grads.append(got[2])
    node_part = grads.pop()
    back = [swap(block, "rep") for block in other] if reps == 2 else [block for block in other]
    later, _ = lax.optimization_barrier((kept, (node_part, back[:-1])))
    mixed = call(
        functools.partial(mix_kernel, total, lookups), "mix", total, (fill,), (dout, v, later), (flat,), micros=40,
    )[0]

    grad_x = call(
        features_kernel, "features", total, (), (features, node_part, swap(node_part, "tp")),
        (shape(BF16, nodes, width),), micros=5,
    )[0]
    if reps == 2:
        ready, _ = lax.optimization_barrier((mine[0], grad_x))
        grad_w = call(
            join_kernel, "join", total, (), (ready, *mine[1:], *back), (shape(F32, 3, share, half_width),),
        )[0]
    else:
        whole = jnp.concatenate([jnp.concatenate(mine, 2), jnp.concatenate(other, 2)], 1)
        whole = jnp.roll(whole, lax.axis_index("rep") * share, 1)
        grad_w = lax.psum_scatter(whole, "rep", scatter_dimension=1, tiled=True)
    return mixed[None], grad_x[None], jnp.transpose(grad_w, (1, 0, 2))


def solution(mesh):
    placed = (
        P(("groups", "rep"), "seq", None),
        P(("groups", "rep"), "seq", "tp"),
        P(None, None, "tp"),
        P(("groups", "rep"), "seq", None),
        P(("groups", "rep"), None),
        P(("groups", "rep"), None),
    )
    return jax.shard_map(
        local,
        mesh=mesh,
        in_specs=placed,
        out_specs=(
            P(("groups", "rep"), "seq", "tp"),
            P(("groups", "rep"), "seq", None),
            P(("groups", "seq", "rep"), None, "tp"),
        ),
        check_vma=False,
    )
```

```python
import functools

import jax
import jax.numpy as jnp
from jax import lax
from jax.experimental import pallas as pl
from jax.experimental.pallas import tpu as pltpu
from jax.sharding import PartitionSpec as P

HDIM = 64
GROUP_VERTICES = 128
PAIR = 2 * HDIM
TAIL = 16
CHUNK = 32
BATCH = 4
NORM_EPS = 1e-06
SCALE = HDIM ** (-0.5)
LOG2E = 1.4426950408889634
F32 = jnp.float32
BF16 = jnp.bfloat16
NT = (((1,), (1,)), ((), ()))
NN = (((1,), (0,)), ((), ()))
TN = (((0,), (0,)), ((), ()))

VMEM = pl.BlockSpec(memory_space=pltpu.VMEM)
SMEM = pl.BlockSpec(memory_space=pltpu.SMEM)


def dot(a, b, dims=NN):
    return lax.dot_general(a, b, dims, preferred_element_type=F32)


def shape(dtype, *sizes):
    return jax.ShapeDtypeStruct(sizes, dtype)


def call(kernel, name, total, scalars, arrays, outs, scratch=(), micros=0):
    return pl.pallas_call(
        kernel,
        out_shape=outs,
        in_specs=[SMEM] * len(scalars) + [VMEM] * len(arrays),
        out_specs=(VMEM,) * len(outs),
        scratch_shapes=scratch,
        compiler_params=pltpu.CompilerParams(vmem_limit_bytes=(10 + 9 * total // 1024) << 20),
        cost_estimate=pl.CostEstimate(flops=micros * 10**9, bytes_accessed=0, transcendentals=0),
        name=name,
    )(*scalars, *arrays)


def prepare_kernel(pairs_ref, cotangent_ref, dout_ref):
    nodes, width = cotangent_ref.shape
    dout_ref[:nodes, :] = cotangent_ref[...]
    row = lax.broadcasted_iota(jnp.int32, (TAIL, width), 0)
    lane = lax.broadcasted_iota(jnp.int32, (TAIL, width), 1)
    tail = jnp.zeros((TAIL, width), F32)
    clusters, lookups = pairs_ref.shape
    for index in range(clusters * lookups):
        entry = pairs_ref[index // lookups, index % lookups].astype(F32)
        tail = jnp.where((row == 0) & (lane == index), entry, tail)
    dout_ref[nodes:, :] = tail.astype(BF16)


def norm(block):
    wide = block.astype(F32)
    inverse = lax.rsqrt(jnp.mean(wide * wide, -1, keepdims=True) + NORM_EPS)
    return (wide * inverse).astype(BF16)


def share_columns(share, width):
    shift = lax.axis_index("rep") * (share // lax.axis_size("rep"))
    index = lax.broadcasted_iota(jnp.int32, (share, width), 0) + shift
    index = jnp.where(index >= share, index - share, index) + lax.axis_index("seq") * share
    columns = lax.broadcasted_iota(jnp.int32, (share, width), 1)
    return jnp.where(columns == index, 1.0, 0.0).astype(BF16)


def project_first_kernel(row_ref, col_ref, w_ref, x_ref, q_ref, k_ref, v_ref, left_ref, put_ref, pick_ref):
    normed = norm(x_ref[...])
    for i, ref in enumerate((q_ref, k_ref, v_ref)):
        ref[...] = dot(normed, w_ref[i]).astype(BF16)
    left_ref[...] = dot(share_columns(*left_ref.shape[:1], normed.shape[1]), normed, NT).astype(BF16)
    places = lax.broadcasted_iota(jnp.int32, put_ref.shape, 0)
    put_ref[...] = jnp.where(places == row_ref[...], 1.0, 0.0).astype(BF16)
    places = lax.broadcasted_iota(jnp.int32, pick_ref.shape, 1)
    pick_ref[...] = jnp.where(places == col_ref[...], 1.0, 0.0).astype(BF16)


def project_next_kernel(w_ref, near_ref, far_ref, q_ref, k_ref, v_ref, left_ref, normed_ref):
    rows = near_ref.shape[0]
    core = lax.axis_index("tp")
    normed_ref[pl.ds(pl.multiple_of(core * rows, rows), rows), :] = norm(near_ref[...])
    normed_ref[pl.ds(pl.multiple_of((1 - core) * rows, rows), rows), :] = norm(far_ref[...])
    normed = normed_ref[...]
    for i, ref in enumerate((q_ref, k_ref, v_ref)):
        ref[...] = dot(normed, w_ref[i]).astype(BF16)
    left_ref[...] = dot(share_columns(*left_ref.shape[:1], normed.shape[1]), normed, NT).astype(BF16)


def project_kernel(shards, w_ref, pick_ref, *refs):
    early, refs = refs[:8], refs[8:]
    near, refs = refs[: shards - 2], refs[shards - 2 :]
    far, refs = refs[: shards - 2], refs[shards - 2 :]
    q_ref, k_ref, v_ref, left_ref, normed_ref = refs
    nodes = early[0].shape[0]
    rows = nodes // 2
    total = shards * nodes
    core = lax.axis_index("tp")
    for i, early_ref in enumerate(early):
        span = slice(i // 4 * nodes, (i // 4 + 1) * nodes)
        if i % 4 == 3:
            left_ref[:, span] = early_ref[...]
        else:
            (q_ref, k_ref, v_ref)[i % 4][span, :] = early_ref[...]
    for shard in range(2, shards):
        mine = pl.multiple_of((shard - 2) * nodes + core * rows, rows)
        other = pl.multiple_of((shard - 2) * nodes + (1 - core) * rows, rows)
        normed_ref[pl.ds(mine, rows), :] = norm(near[shard - 2][...])
        normed_ref[pl.ds(other, rows), :] = norm(far[shard - 2][...])
    columns = share_columns(left_ref.shape[0], normed_ref.shape[1])
    for start in range(2 * nodes, total, BATCH * nodes):
        stop = min(start + BATCH * nodes, total)
        normed = normed_ref[start - 2 * nodes : stop - 2 * nodes, :]
        for i, ref in enumerate((q_ref, k_ref, v_ref)):
            ref[start:stop, :] = dot(normed, w_ref[i]).astype(BF16)
        left_ref[:, start:stop] = dot(columns, normed, NT).astype(BF16)
    key_sum = value_sum = None
    for start in range(0, total, BATCH * nodes):
        stop = min(start + BATCH * nodes, total)
        pick = pick_ref[:, start:stop]
        keys, values = dot(pick, k_ref[start:stop, :]), dot(pick, v_ref[start:stop, :])
        key_sum = keys if start == 0 else key_sum + keys
        value_sum = values if start == 0 else value_sum + values
    k_ref[total:, :] = key_sum.astype(BF16)
    v_ref[total:, :] = value_sum.astype(BF16)


def read_pairs(fill_ref, dout_ref, nodes, clusters, lookups):
    tail = dout_ref[nodes:, :PAIR].astype(F32)
    lane = lax.broadcasted_iota(jnp.int32, tail.shape, 1)
    base = fill_ref.shape[0]
    weight = jnp.zeros(tail.shape, F32)
    for index in range(clusters * lookups):
        weight = jnp.where(lane == index, float(base**index), weight)
    code = jnp.sum(tail * weight).astype(jnp.int32)
    me = lax.axis_index("seq")
    entries = []
    for index in range(clusters * lookups):
        cluster = lax.rem(lax.div(code, base**index), base)
        block = (lax.div(cluster, clusters) ^ me) * clusters + lax.rem(cluster, clusters)
        entries.append((pl.multiple_of(block * GROUP_VERTICES, GROUP_VERTICES), fill_ref[cluster]))
    return [entries[i * lookups : (i + 1) * lookups] for i in range(clusters)]


def fold(block, op):
    result = block[:8]
    for start in range(8, block.shape[0], 8):
        result = op(result, block[start : start + 8])
    return result


def unit(slot, shard, total, entries, cluster, column, refs, accs, acc_cols, emit, scratch):
    q_ref, dout_ref, k_ref, v_ref = refs
    score_ref, dprob_ref, prob_ref, dscore_ref = (ref.at[slot] for ref in scratch)
    dk_ref, dv_ref = accs
    size = GROUP_VERTICES
    clusters = (dout_ref.shape[0] - TAIL) // size
    local_rows = len(entries) * size
    listed = local_rows + k_ref.shape[0] - total
    cols = slice(column, column + PAIR)
    state = {}
    places = [pl.ds(start, size) for start, _ in entries]
    places += [pl.ds(start, size) for start in range(total, k_ref.shape[0], size)]

    def split(block):
        low = lax.broadcasted_iota(jnp.int32, (size, PAIR), 1) < HDIM
        zero = jnp.zeros((), BF16)
        return jnp.concatenate([jnp.where(low, block, zero), jnp.where(low, zero, block)], 0)

    def load():
        start = (shard * clusters + cluster) * size
        real = lax.broadcasted_iota(jnp.int32, (size, 1), 0) < entries[0][1]
        douts = dout_ref[cluster * size : (cluster + 1) * size, cols]
        state["queries"] = split(q_ref[start : start + size, cols])
        state["douts"] = split(jnp.where(real, douts, jnp.zeros((), BF16)))

    def score_step(index):
        span = slice(index * size, (index + 1) * size)
        score_ref[span, :] = dot(k_ref[places[index], cols], state["queries"], NT)

    def dprob_step(index):
        span = slice(index * size, (index + 1) * size)
        dprob_ref[span, :] = dot(v_ref[places[index], cols], state["douts"], NT)

    def masked(start):
        block = score_ref[start : start + CHUNK, :]
        if start >= local_rows:
            return block
        slots = lax.broadcasted_iota(jnp.int32, (CHUNK, 2 * size), 0) + start % size
        return jnp.where(slots < entries[start // size][1], block, -1e30)

    def peak_step(start):
        part = fold(masked(start), jnp.maximum)
        state["peak"] = part if start == 0 else jnp.maximum(state["peak"], part)

    def term_step(start):
        if start == 0:
            state["peak"] = jnp.max(state["peak"], 0, keepdims=True)
        terms = jnp.exp2((masked(start) - state["peak"]) * (LOG2E * SCALE))
        weighted = fold(terms * dprob_ref[start : start + CHUNK, :], jnp.add)
        score_ref[start : start + CHUNK, :] = terms
        terms = fold(terms, jnp.add)
        state["sum"] = terms if start == 0 else state["sum"] + terms
        state["weighted"] = weighted if start == 0 else state["weighted"] + weighted

    def prob_step(start):
        if start == 0:
            state["inverse"] = 1.0 / jnp.sum(state["sum"], 0, keepdims=True)
            state["delta"] = jnp.sum(state["weighted"], 0, keepdims=True) * state["inverse"]
        span = slice(start, start + CHUNK)
        prob = score_ref[span, :] * state["inverse"]
        prob_ref[span, :] = prob.astype(BF16)
        dscore_ref[span, :] = (prob * (dprob_ref[span, :] - state["delta"])).astype(BF16)

    def value_step(index):
        span = slice(index * size, (index + 1) * size)
        dv_ref[places[index], acc_cols] += dot(prob_ref[span, :], state["douts"])

    def key_step(index):
        span = slice(index * size, (index + 1) * size)
        dk_ref[places[index], acc_cols] += dot(dscore_ref[span, :], state["queries"]) * SCALE

    def query_step():
        keys = jnp.concatenate([k_ref[place, cols] for place in places], 0)
        emit(cluster, column, joined(dot(keys, dscore_ref[...], TN) * SCALE).astype(BF16), prob_ref)

    step = functools.partial
    blocks, chunks = range(listed // size), range(0, listed, CHUNK)
    ahead = [load] + [step(f, i) for i in blocks for f in (score_step, dprob_step)]
    middle = [step(f, start) for f in (peak_step, term_step, prob_step) for start in chunks]
    behind = [step(f, i) for i in blocks for f in (value_step, key_step)] + [query_step]
    return ahead, middle, behind


def joined(block):
    size = GROUP_VERTICES
    return jnp.concatenate([block[:HDIM, :size], block[HDIM:, size:]], 0).T


def run_units(units):
    for step in units[0][0]:
        step()
    for index, (_, middle, _) in enumerate(units):
        beside = units[index - 1][2] if index else []
        beside = beside + (units[index + 1][0] if index + 1 < len(units) else [])
        done = 0
        for position, step in enumerate(middle):
            step()
            while done < (position + 1) * len(beside) // len(middle):
                beside[done]()
                done += 1
    for step in units[-1][2]:
        step()


def attend_kernel(group, total, lookups, first, fill_ref, q_ref, k_ref, v_ref, *refs):
    scratch, refs = refs[-4:], refs[:-4]
    dout_refs, refs = refs[: len(group)], refs[len(group) :]
    if first:
        dk_ref, dv_ref, probs_ref, *dq_refs = refs
        dk_ref[...] = jnp.zeros_like(dk_ref)
        dv_ref[...] = jnp.zeros_like(dv_ref)
    else:
        dk_in, dv_in, dk_ref, dv_ref, *dq_refs = refs
        dk_ref[...] = dk_in[...]
        dv_ref[...] = dv_in[...]
    nodes, width = dq_refs[0].shape
    clusters = nodes // GROUP_VERTICES

    def emit_to(shard, dq_ref):
        def emit(cluster, column, dq, prob_ref):
            dq_ref[cluster * GROUP_VERTICES : (cluster + 1) * GROUP_VERTICES, column : column + PAIR] = dq
            if shard == 0:
                probs_ref[cluster * (width // PAIR) + column // PAIR] = prob_ref[...]

        return emit

    units = []
    for shard, dout_ref, dq_ref in zip(group, dout_refs, dq_refs):
        entries = read_pairs(fill_ref, dout_ref, nodes, clusters, lookups)
        for cluster in range(clusters):
            for column in range(0, width, PAIR):
                units.append(
                    unit(
                        len(units) % 2, shard, total, entries[cluster], cluster, column,
                        (q_ref, dout_ref, k_ref, v_ref), (dk_ref, dv_ref),
                        slice(column, column + PAIR), emit_to(shard, dq_ref), scratch,
                    )
                )
    run_units(units)


def mix_kernel(total, lookups, fill_ref, dout_ref, v_ref, probs_ref, out_ref):
    size = GROUP_VERTICES
    nodes, width = out_ref.shape
    clusters = nodes // size
    entries = read_pairs(fill_ref, dout_ref, nodes, clusters, lookups)
    for cluster in range(clusters):
        real = lax.broadcasted_iota(jnp.int32, (size, 1), 0) < entries[cluster][0][1]
        for column in range(0, width, PAIR):
            cols = slice(column, column + PAIR)
            values = [v_ref[pl.ds(start, size), cols] for start, _ in entries[cluster]]
            values = jnp.concatenate(values + [v_ref[total:, cols]], 0)
            probs = probs_ref[cluster * (width // PAIR) + column // PAIR]
            mixed = jnp.where(real, joined(dot(values, probs, TN)), 0.0)
            out_ref[cluster * size : (cluster + 1) * size, cols] = mixed.astype(BF16)


def finish_kernel(shard, shards, total, lookups, column, final, fill_ref, q_ref, dout_ref, k_ref, v_ref, *refs):
    scratch, refs = refs[-4:], refs[:-4]
    dk_in, dv_in, left_ref, put_ref = refs[:4]
    dq_refs, refs = refs[4 : 3 + shards], refs[3 + shards :]
    own_refs = []
    if final:
        w_ref, own_refs, refs = refs[0], list(refs[1 : 1 + column // PAIR]), refs[1 + column // PAIR :]
    mine_ref, other_ref, own_ref, dk_ref, dv_ref, dq_ref, all_ref = refs
    cols = slice(column, column + PAIR)
    dk_ref[...] = dk_in[:, cols]
    dv_ref[...] = dv_in[:, cols]
    nodes = dq_ref.shape[0]
    clusters = nodes // GROUP_VERTICES
    entries = read_pairs(fill_ref, dout_ref, nodes, clusters, lookups)

    def emit(cluster, column, dq, prob_ref):
        dq_ref[cluster * GROUP_VERTICES : (cluster + 1) * GROUP_VERTICES, :] = dq

    run_units(
        [
            unit(
                cluster % 2, shard, total, entries[cluster], cluster, column,
                (q_ref, dout_ref, k_ref, v_ref), (dk_ref, dv_ref), slice(0, PAIR), emit, scratch,
            )
            for cluster in range(clusters)
        ]
    )
    share = mine_ref.shape[1]
    wide = jnp.concatenate([dk_ref[total:, :], dv_ref[total:, :]], 1)
    high = wide.astype(BF16)
    picked = jnp.concatenate([high, (wide - high.astype(F32)).astype(BF16)], 0)
    order = iter(dq_refs)
    for block in range(shards):
        span = slice(block * nodes, (block + 1) * nodes)
        put = put_ref[span, :]
        added = dot(jnp.concatenate([put, put], 1), picked)
        all_ref[span, :PAIR] = dq_ref[...] if block == shard else next(order)[:, cols]
        all_ref[span, PAIR : 2 * PAIR] = (dk_ref[span, :] + added[:, :PAIR]).astype(BF16)
        all_ref[span, 2 * PAIR :] = (dv_ref[span, :] + added[:, PAIR:]).astype(BF16)
    sums = None
    for start in range(0, total, BATCH * nodes):
        stop = min(start + BATCH * nodes, total)
        term = dot(left_ref[:, start:stop], all_ref[start:stop, :])
        sums = term if start == 0 else sums + term
    for i in range(3):
        mine_ref[i] = sums[:share, i * PAIR : (i + 1) * PAIR]
        other_ref[i] = sums[share:, i * PAIR : (i + 1) * PAIR]
    if not final:
        own_ref[...] = all_ref[:nodes, :]
        return
    node = None
    for i in range(3):
        part = slice(i * PAIR, (i + 1) * PAIR)
        grads = [ref[:, part] for ref in own_refs] + [all_ref[:nodes, part]]
        term = dot(jnp.concatenate(grads, 1), w_ref[i], NT)
        node = term if node is None else node + term
    own_ref[...] = node


def features_kernel(x_ref, mine_ref, other_ref, out_ref):
    wide = x_ref[...].astype(F32)
    inverse = lax.rsqrt(jnp.mean(wide * wide, -1, keepdims=True) + NORM_EPS)
    normed = wide * inverse
    grad = mine_ref[...] + other_ref[...]
    out_ref[...] = (inverse * (grad - normed * jnp.mean(normed * grad, -1, keepdims=True))).astype(BF16)


def join_kernel(*refs):
    out_ref = refs[-1]
    half = (len(refs) - 1) // 2
    for index in range(half):
        cols = slice(index * PAIR, (index + 1) * PAIR)
        out_ref[:, :, cols] = refs[index][...] + refs[half + index][...]


def local(node_features, result_cotangent, proj_weights, cluster_pairs, cluster_fill, global_nodes):
    features = node_features[0]
    cotangent = result_cotangent[0]
    pairs = cluster_pairs[0]
    fill = cluster_fill[0]
    global_ids = global_nodes[0]
    weights = jnp.transpose(proj_weights, (1, 0, 2))
    nodes, width = features.shape
    half_width = cotangent.shape[1]
    lookups = pairs.shape[1]
    shards = lax.axis_size("seq")
    reps = lax.axis_size("rep")
    me = lax.axis_index("seq")
    total = shards * nodes
    count = global_ids.shape[0]
    share = width // (shards * reps)

    def trade(value, step):
        return lax.ppermute(value, "seq", [(j, j ^ step) for j in range(shards)])

    def swap(value, axis):
        return lax.ppermute(value, axis, [(0, 1), (1, 0)])

    half = lax.dynamic_slice_in_dim(features, lax.axis_index("tp") * (nodes // 2), nodes // 2)
    steps = [1] + list(range(shards - 1, 1, -1))
    near = {step: trade(half, step) for step in steps}
    far = {1: swap(near[1], "tp")}
    dout = call(
        prepare_kernel, "prepare", total, (pairs,), (cotangent,), (shape(BF16, nodes + TAIL, half_width),),
        micros=1,
    )[0]
    douts = {0: dout, 1: trade(dout, 1)}
    ids = ((global_ids // nodes) ^ me) * nodes + global_ids % nodes
    flat = shape(BF16, nodes, half_width)
    columns = shape(BF16, reps * share, nodes)
    *first, put, pick = call(
        project_first_kernel, "project_first", total, (),
        (ids[None, :], ids[:, None], weights, features),
        (flat, flat, flat, columns, shape(BF16, total, count), shape(BF16, count, total)), micros=2,
    )
    second = call(
        project_next_kernel, "project_next", total, (), (weights, near[1], far[1]),
        (flat, flat, flat, columns), (pltpu.VMEM((nodes, width), BF16),), micros=2,
    )
    for step in steps[1:]:
        near[step], _ = lax.optimization_barrier((near[step], (first[0], second[0])))
        far[step] = swap(near[step], "tp")
        ready, _ = lax.optimization_barrier((dout, near[step]))
        douts[step] = trade(ready, step)
    q, k, v, left = call(
        functools.partial(project_kernel, shards), "project", total, (),
        (weights, pick, *first, *second, *[near[i] for i in range(2, shards)], *[far[i] for i in range(2, shards)]),
        (
            shape(BF16, total, half_width),
            shape(BF16, total + count, half_width),
            shape(BF16, total + count, half_width),
            shape(BF16, reps * share, total),
        ),
        (pltpu.VMEM((total - 2 * nodes, width), BF16),),
    )

    acc = shape(F32, total + count, half_width)
    listed = lookups * GROUP_VERTICES + count
    grid = (listed, 2 * GROUP_VERTICES)
    probs = shape(BF16, nodes // GROUP_VERTICES * (half_width // PAIR), *grid)
    scratch = tuple(pltpu.VMEM((2,) + grid, kind) for kind in (F32, F32, BF16, BF16))
    dqs = {}
    dk = dv = kept = None
    for group in [[0] + steps[:1]] + [[step] for step in steps[1:-1]]:
        first = 0 in group
        got = call(
            functools.partial(attend_kernel, group, total, lookups, first), "attend_%d" % group[-1], total,
            (fill,), (q, k, v, *[douts[i] for i in group]) + (() if first else (dk, dv)),
            (acc, acc) + ((probs,) if first else ()) + (flat,) * len(group), scratch,
        )
        dk, dv = got[:2]
        kept = got[2] if first else kept
        dqs.update(zip(group, got[-len(group) :]))
    last = steps[-1]
    mine, other, grads = [], [], []
    for column in range(0, half_width, PAIR):
        final = column + PAIR == half_width
        got = call(
            functools.partial(finish_kernel, last, shards, total, lookups, column, final),
            "finish_%d" % column, total, (fill,),
            (q, douts[last], k, v, dk, dv, left, put)
            + tuple(dqs[i] for i in sorted(dqs)) + ((weights, *grads) if final else ()),
            (
                shape(F32, 3, share, PAIR),
                shape(F32, 3, (reps - 1) * share, PAIR),
                shape(F32, nodes, width) if final else shape(BF16, nodes, 3 * PAIR),
            ),
            (
                pltpu.VMEM((total + count, PAIR), F32),
                pltpu.VMEM((total + count, PAIR), F32),
                pltpu.VMEM((nodes, PAIR), BF16),
                pltpu.VMEM((total, 3 * PAIR), BF16),
            ) + scratch,
        )
        mine.append(got[0])
        other.append(got[1])
        grads.append(got[2])
    node_part = grads.pop()
    back = [swap(block, "rep") for block in other] if reps == 2 else [block for block in other]
    later, _ = lax.optimization_barrier((kept, (node_part, back[:-1])))
    mixed = call(
        functools.partial(mix_kernel, total, lookups), "mix", total, (fill,), (dout, v, later), (flat,), micros=40,
    )[0]

    grad_x = call(
        features_kernel, "features", total, (), (features, node_part, swap(node_part, "tp")),
        (shape(BF16, nodes, width),), micros=5,
    )[0]
    if reps == 2:
        ready, _ = lax.optimization_barrier((mine[0], grad_x))
        grad_w = call(
            join_kernel, "join", total, (), (ready, *mine[1:], *back), (shape(F32, 3, share, half_width),),
        )[0]
    else:
        whole = jnp.concatenate([jnp.concatenate(mine, 2), jnp.concatenate(other, 2)], 1)
        whole = jnp.roll(whole, lax.axis_index("rep") * share, 1)
        grad_w = lax.psum_scatter(whole, "rep", scatter_dimension=1, tiled=True)
    return mixed[None], grad_x[None], jnp.transpose(grad_w, (1, 0, 2))


def solution(mesh):
    placed = (
        P(("groups", "rep"), "seq", None),
        P(("groups", "rep"), "seq", "tp"),
        P(None, None, "tp"),
        P(("groups", "rep"), "seq", None),
        P(("groups", "rep"), None),
        P(("groups", "rep"), None),
    )
    return jax.shard_map(
        local,
        mesh=mesh,
        in_specs=placed,
        out_specs=(
            P(("groups", "rep"), "seq", "tp"),
            P(("groups", "rep"), "seq", None),
            P(("groups", "seq", "rep"), None, "tp"),
        ),
        check_vma=False,
    )
```

```python
import functools

import jax
import jax.numpy as jnp
from jax import lax
from jax.experimental import pallas as pl
from jax.experimental.pallas import tpu as pltpu
from jax.sharding import PartitionSpec as P

HDIM = 64
GROUP_VERTICES = 128
PAIR = 2 * HDIM
TAIL = 16
CHUNK = 32
BATCH = 4
NORM_EPS = 1e-06
SCALE = HDIM ** (-0.5)
LOG2E = 1.4426950408889634
F32 = jnp.float32
BF16 = jnp.bfloat16
NT = (((1,), (1,)), ((), ()))
NN = (((1,), (0,)), ((), ()))
TN = (((0,), (0,)), ((), ()))

VMEM = pl.BlockSpec(memory_space=pltpu.VMEM)
SMEM = pl.BlockSpec(memory_space=pltpu.SMEM)


def dot(a, b, dims=NN):
    return lax.dot_general(a, b, dims, preferred_element_type=F32)


def shape(dtype, *sizes):
    return jax.ShapeDtypeStruct(sizes, dtype)


def call(kernel, name, total, scalars, arrays, outs, scratch=(), micros=0):
    return pl.pallas_call(
        kernel,
        out_shape=outs,
        in_specs=[SMEM] * len(scalars) + [VMEM] * len(arrays),
        out_specs=(VMEM,) * len(outs),
        scratch_shapes=scratch,
        compiler_params=pltpu.CompilerParams(vmem_limit_bytes=(10 + 9 * total // 1024) << 20),
        cost_estimate=pl.CostEstimate(flops=micros * 10**9, bytes_accessed=0, transcendentals=0),
        name=name,
    )(*scalars, *arrays)


def prepare_kernel(pairs_ref, cotangent_ref, dout_ref):
    nodes, width = cotangent_ref.shape
    dout_ref[:nodes, :] = cotangent_ref[...]
    row = lax.broadcasted_iota(jnp.int32, (TAIL, width), 0)
    lane = lax.broadcasted_iota(jnp.int32, (TAIL, width), 1)
    tail = jnp.zeros((TAIL, width), F32)
    clusters, lookups = pairs_ref.shape
    for index in range(clusters * lookups):
        entry = pairs_ref[index // lookups, index % lookups].astype(F32)
        tail = jnp.where((row == 0) & (lane == index), entry, tail)
    dout_ref[nodes:, :] = tail.astype(BF16)


def norm(block):
    wide = block.astype(F32)
    inverse = lax.rsqrt(jnp.mean(wide * wide, -1, keepdims=True) + NORM_EPS)
    return (wide * inverse).astype(BF16)


def share_columns(share, width):
    shift = lax.axis_index("rep") * (share // lax.axis_size("rep"))
    index = lax.broadcasted_iota(jnp.int32, (share, width), 0) + shift
    index = jnp.where(index >= share, index - share, index) + lax.axis_index("seq") * share
    columns = lax.broadcasted_iota(jnp.int32, (share, width), 1)
    return jnp.where(columns == index, 1.0, 0.0).astype(BF16)


def project_first_kernel(row_ref, col_ref, w_ref, x_ref, q_ref, k_ref, v_ref, left_ref, put_ref, pick_ref):
    normed = norm(x_ref[...])
    for i, ref in enumerate((q_ref, k_ref, v_ref)):
        ref[...] = dot(normed, w_ref[i]).astype(BF16)
    left_ref[...] = dot(share_columns(*left_ref.shape[:1], normed.shape[1]), normed, NT).astype(BF16)
    places = lax.broadcasted_iota(jnp.int32, put_ref.shape, 0)
    put_ref[...] = jnp.where(places == row_ref[...], 1.0, 0.0).astype(BF16)
    places = lax.broadcasted_iota(jnp.int32, pick_ref.shape, 1)
    pick_ref[...] = jnp.where(places == col_ref[...], 1.0, 0.0).astype(BF16)


def project_next_kernel(w_ref, near_ref, far_ref, q_ref, k_ref, v_ref, left_ref, normed_ref):
    rows = near_ref.shape[0]
    core = lax.axis_index("tp")
    normed_ref[pl.ds(pl.multiple_of(core * rows, rows), rows), :] = norm(near_ref[...])
    normed_ref[pl.ds(pl.multiple_of((1 - core) * rows, rows), rows), :] = norm(far_ref[...])
    normed = normed_ref[...]
    for i, ref in enumerate((q_ref, k_ref, v_ref)):
        ref[...] = dot(normed, w_ref[i]).astype(BF16)
    left_ref[...] = dot(share_columns(*left_ref.shape[:1], normed.shape[1]), normed, NT).astype(BF16)


def project_kernel(shards, w_ref, pick_ref, *refs):
    early, refs = refs[:8], refs[8:]
    near, refs = refs[: shards - 2], refs[shards - 2 :]
    far, refs = refs[: shards - 2], refs[shards - 2 :]
    q_ref, k_ref, v_ref, left_ref, normed_ref = refs
    nodes = early[0].shape[0]
    rows = nodes // 2
    total = shards * nodes
    core = lax.axis_index("tp")
    for i, early_ref in enumerate(early):
        span = slice(i // 4 * nodes, (i // 4 + 1) * nodes)
        if i % 4 == 3:
            left_ref[:, span] = early_ref[...]
        else:
            (q_ref, k_ref, v_ref)[i % 4][span, :] = early_ref[...]
    for shard in range(2, shards):
        mine = pl.multiple_of((shard - 2) * nodes + core * rows, rows)
        other = pl.multiple_of((shard - 2) * nodes + (1 - core) * rows, rows)
        normed_ref[pl.ds(mine, rows), :] = norm(near[shard - 2][...])
        normed_ref[pl.ds(other, rows), :] = norm(far[shard - 2][...])
    columns = share_columns(left_ref.shape[0], normed_ref.shape[1])
    for start in range(2 * nodes, total, BATCH * nodes):
        stop = min(start + BATCH * nodes, total)
        normed = normed_ref[start - 2 * nodes : stop - 2 * nodes, :]
        for i, ref in enumerate((q_ref, k_ref, v_ref)):
            ref[start:stop, :] = dot(normed, w_ref[i]).astype(BF16)
        left_ref[:, start:stop] = dot(columns, normed, NT).astype(BF16)
    key_sum = value_sum = None
    for start in range(0, total, BATCH * nodes):
        stop = min(start + BATCH * nodes, total)
        pick = pick_ref[:, start:stop]
        keys, values = dot(pick, k_ref[start:stop, :]), dot(pick, v_ref[start:stop, :])
        key_sum = keys if start == 0 else key_sum + keys
        value_sum = values if start == 0 else value_sum + values
    k_ref[total:, :] = key_sum.astype(BF16)
    v_ref[total:, :] = value_sum.astype(BF16)


def read_pairs(fill_ref, dout_ref, nodes, clusters, lookups):
    tail = dout_ref[nodes:, :PAIR].astype(F32)
    lane = lax.broadcasted_iota(jnp.int32, tail.shape, 1)
    bits = (fill_ref.shape[0] - 1).bit_length()
    weight = jnp.zeros(tail.shape, F32)
    for index in range(clusters * lookups):
        weight = jnp.where(lane == index, float(1 << bits * index), weight)
    code = jnp.sum(tail * weight).astype(jnp.int32)
    me = lax.axis_index("seq")
    entries = []
    for index in range(clusters * lookups):
        cluster = (code >> (bits * index)) & ((1 << bits) - 1)
        place = clusters.bit_length() - 1
        block = ((cluster >> place) ^ me) * clusters + (cluster & (clusters - 1))
        entries.append((pl.multiple_of(block * GROUP_VERTICES, GROUP_VERTICES), fill_ref[cluster]))
    return [entries[i * lookups : (i + 1) * lookups] for i in range(clusters)]


def fold(block, op):
    result = block[:8]
    for start in range(8, block.shape[0], 8):
        result = op(result, block[start : start + 8])
    return result


def unit(slot, shard, total, entries, cluster, column, refs, accs, acc_cols, emit, scratch):
    q_ref, dout_ref, k_ref, v_ref = refs
    score_ref, dprob_ref, prob_ref, dscore_ref = (ref.at[slot] for ref in scratch)
    dk_ref, dv_ref = accs
    size = GROUP_VERTICES
    clusters = (dout_ref.shape[0] - TAIL) // size
    listed = len(entries) * size + k_ref.shape[0] - total
    cols = slice(column, column + PAIR)
    state = {}
    places = [pl.ds(start, size) for start, _ in entries]
    places += [pl.ds(start, size) for start in range(total, k_ref.shape[0], size)]

    def split(block):
        low = lax.broadcasted_iota(jnp.int32, (size, PAIR), 1) < HDIM
        zero = jnp.zeros((), BF16)
        return jnp.concatenate([jnp.where(low, block, zero), jnp.where(low, zero, block)], 0)

    def load():
        start = (shard * clusters + cluster) * size
        real = lax.broadcasted_iota(jnp.int32, (size, 1), 0) < entries[0][1]
        douts = dout_ref[cluster * size : (cluster + 1) * size, cols]
        state["queries"] = split(q_ref[start : start + size, cols])
        state["douts"] = split(jnp.where(real, douts, jnp.zeros((), BF16)))

    def score_step(index):
        span = slice(index * size, (index + 1) * size)
        scores = dot(k_ref[places[index], cols], state["queries"], NT)
        if index < len(entries):
            slots = lax.broadcasted_iota(jnp.int32, scores.shape, 0)
            scores = jnp.where(slots < entries[index][1], scores, -1e30)
        score_ref[span, :] = scores

    def dprob_step(index):
        span = slice(index * size, (index + 1) * size)
        dprob_ref[span, :] = dot(v_ref[places[index], cols], state["douts"], NT)

    def peak_step(start):
        part = fold(score_ref[start : start + CHUNK, :], jnp.maximum)
        state["peak"] = part if start == 0 else jnp.maximum(state["peak"], part)

    def term_step(start):
        if start == 0:
            state["peak"] = jnp.max(state["peak"], 0, keepdims=True)
        terms = jnp.exp2((score_ref[start : start + CHUNK, :] - state["peak"]) * (LOG2E * SCALE))
        weighted = fold(terms * dprob_ref[start : start + CHUNK, :], jnp.add)
        score_ref[start : start + CHUNK, :] = terms
        terms = fold(terms, jnp.add)
        state["sum"] = terms if start == 0 else state["sum"] + terms
        state["weighted"] = weighted if start == 0 else state["weighted"] + weighted

    def prob_step(start):
        if start == 0:
            state["inverse"] = 1.0 / jnp.sum(state["sum"], 0, keepdims=True)
            state["delta"] = jnp.sum(state["weighted"], 0, keepdims=True) * state["inverse"]
        span = slice(start, start + CHUNK)
        prob = score_ref[span, :] * state["inverse"]
        prob_ref[span, :] = prob.astype(BF16)
        dscore_ref[span, :] = (prob * (dprob_ref[span, :] - state["delta"])).astype(BF16)

    def value_step(index):
        span = slice(index * size, (index + 1) * size)
        dv_ref[places[index], acc_cols] += dot(prob_ref[span, :], state["douts"])

    def key_step(index):
        span = slice(index * size, (index + 1) * size)
        dk_ref[places[index], acc_cols] += dot(dscore_ref[span, :], state["queries"]) * SCALE

    def query_step():
        keys = jnp.concatenate([k_ref[place, cols] for place in places], 0)
        emit(cluster, column, joined(dot(keys, dscore_ref[...], TN) * SCALE).astype(BF16), prob_ref)

    step = functools.partial
    blocks, chunks = range(listed // size), range(0, listed, CHUNK)
    ahead = [load] + [step(f, i) for i in blocks for f in (score_step, dprob_step)]
    middle = [step(f, start) for f in (peak_step, term_step, prob_step) for start in chunks]
    behind = [step(f, i) for i in blocks for f in (value_step, key_step)] + [query_step]
    return ahead, middle, behind


def joined(block):
    size = GROUP_VERTICES
    return jnp.concatenate([block[:HDIM, :size], block[HDIM:, size:]], 0).T


def run_units(units):
    for step in units[0][0]:
        step()
    for index, (_, middle, _) in enumerate(units):
        beside = units[index - 1][2] if index else []
        beside = beside + (units[index + 1][0] if index + 1 < len(units) else [])
        done = 0
        for position, step in enumerate(middle):
            step()
            while done < (position + 1) * len(beside) // len(middle):
                beside[done]()
                done += 1
    for step in units[-1][2]:
        step()


def attend_kernel(group, total, lookups, first, fill_ref, q_ref, k_ref, v_ref, *refs):
    scratch, refs = refs[-4:], refs[:-4]
    dout_refs, refs = refs[: len(group)], refs[len(group) :]
    if first:
        dk_ref, dv_ref, probs_ref, *dq_refs = refs
        dk_ref[...] = jnp.zeros_like(dk_ref)
        dv_ref[...] = jnp.zeros_like(dv_ref)
    else:
        dk_in, dv_in, dk_ref, dv_ref, *dq_refs = refs
        dk_ref[...] = dk_in[...]
        dv_ref[...] = dv_in[...]
    nodes, width = dq_refs[0].shape
    clusters = nodes // GROUP_VERTICES

    def emit_to(shard, dq_ref):
        def emit(cluster, column, dq, prob_ref):
            dq_ref[cluster * GROUP_VERTICES : (cluster + 1) * GROUP_VERTICES, column : column + PAIR] = dq
            if shard == 0:
                probs_ref[cluster * (width // PAIR) + column // PAIR] = prob_ref[...]

        return emit

    units = []
    for shard, dout_ref, dq_ref in zip(group, dout_refs, dq_refs):
        entries = read_pairs(fill_ref, dout_ref, nodes, clusters, lookups)
        for cluster in range(clusters):
            for column in range(0, width, PAIR):
                units.append(
                    unit(
                        len(units) % 2, shard, total, entries[cluster], cluster, column,
                        (q_ref, dout_ref, k_ref, v_ref), (dk_ref, dv_ref),
                        slice(column, column + PAIR), emit_to(shard, dq_ref), scratch,
                    )
                )
    run_units(units)


def share_product(left_ref, all_ref, begin, end):
    aligned = begin % TAIL == 0 and end % TAIL == 0
    total = all_ref.shape[0]
    sums = None
    for start in range(0, total, 1024):
        stop = min(start + 1024, total)
        left = left_ref[begin:end, start:stop] if aligned else left_ref[:, start:stop]
        term = dot(left, all_ref[start:stop, :])
        sums = term if start == 0 else sums + term
    return sums if aligned else sums[begin:end]


def mix_kernel(total, lookups, fill_ref, dout_ref, v_ref, probs_ref, left_ref, *refs):
    *all_refs, out_ref, mine_ref = refs
    for index, all_ref in enumerate(all_refs):
        sums = share_product(left_ref, all_ref, 0, mine_ref.shape[1])
        for i in range(3):
            mine_ref[i, :, index * PAIR : (index + 1) * PAIR] = sums[:, i * PAIR : (i + 1) * PAIR]
    size = GROUP_VERTICES
    nodes, width = out_ref.shape
    clusters = nodes // size
    entries = read_pairs(fill_ref, dout_ref, nodes, clusters, lookups)
    for cluster in range(clusters):
        real = lax.broadcasted_iota(jnp.int32, (size, 1), 0) < entries[cluster][0][1]
        for column in range(0, width, PAIR):
            cols = slice(column, column + PAIR)
            values = [v_ref[pl.ds(start, size), cols] for start, _ in entries[cluster]]
            values = jnp.concatenate(values + [v_ref[total:, cols]], 0)
            probs = probs_ref[cluster * (width // PAIR) + column // PAIR]
            mixed = jnp.where(real, joined(dot(values, probs, TN)), 0.0)
            out_ref[cluster * size : (cluster + 1) * size, cols] = mixed.astype(BF16)


def finish_kernel(shard, shards, total, lookups, column, final, fill_ref, q_ref, dout_ref, k_ref, v_ref, *refs):
    scratch, refs = refs[-4:], refs[:-4]
    dk_in, dv_in, left_ref, put_ref = refs[:4]
    dq_refs, refs = refs[4 : 3 + shards], refs[3 + shards :]
    own_refs = []
    if final:
        w_ref, own_refs, refs = refs[0], list(refs[1 : 1 + column // PAIR]), refs[1 + column // PAIR :]
    other_ref, all_ref, *node_refs, dk_ref, dv_ref, dq_ref = refs
    cols = slice(column, column + PAIR)
    dk_ref[...] = dk_in[:, cols]
    dv_ref[...] = dv_in[:, cols]
    nodes = dq_ref.shape[0]
    clusters = nodes // GROUP_VERTICES
    entries = read_pairs(fill_ref, dout_ref, nodes, clusters, lookups)

    def emit(cluster, column, dq, prob_ref):
        dq_ref[cluster * GROUP_VERTICES : (cluster + 1) * GROUP_VERTICES, :] = dq

    run_units(
        [
            unit(
                cluster % 2, shard, total, entries[cluster], cluster, column,
                (q_ref, dout_ref, k_ref, v_ref), (dk_ref, dv_ref), slice(0, PAIR), emit, scratch,
            )
            for cluster in range(clusters)
        ]
    )
    share = left_ref.shape[0] - other_ref.shape[1]
    wide = jnp.concatenate([dk_ref[total:, :], dv_ref[total:, :]], 1)
    high = wide.astype(BF16)
    picked = jnp.concatenate([high, (wide - high.astype(F32)).astype(BF16)], 0)
    order = iter(dq_refs)
    for block in range(shards):
        span = slice(block * nodes, (block + 1) * nodes)
        put = put_ref[span, :]
        added = dot(jnp.concatenate([put, put], 1), picked)
        all_ref[span, :PAIR] = dq_ref[...] if block == shard else next(order)[:, cols]
        all_ref[span, PAIR : 2 * PAIR] = (dk_ref[span, :] + added[:, :PAIR]).astype(BF16)
        all_ref[span, 2 * PAIR :] = (dv_ref[span, :] + added[:, PAIR:]).astype(BF16)
    sums = share_product(left_ref, all_ref, share, left_ref.shape[0])
    for i in range(3):
        other_ref[i] = sums[:, i * PAIR : (i + 1) * PAIR]
    if not final:
        return
    node = None
    for i in range(3):
        part = slice(i * PAIR, (i + 1) * PAIR)
        grads = [ref[:nodes, part] for ref in own_refs] + [all_ref[:nodes, part]]
        term = dot(jnp.concatenate(grads, 1), w_ref[i], NT)
        node = term if node is None else node + term
    node_refs[0][...] = node


def features_kernel(x_ref, mine_ref, other_ref, out_ref):
    wide = x_ref[...].astype(F32)
    inverse = lax.rsqrt(jnp.mean(wide * wide, -1, keepdims=True) + NORM_EPS)
    normed = wide * inverse
    grad = mine_ref[...] + other_ref[...]
    out_ref[...] = (inverse * (grad - normed * jnp.mean(normed * grad, -1, keepdims=True))).astype(BF16)


def join_kernel(mine_ref, *refs):
    out_ref = refs[-1]
    for index, back_ref in enumerate(refs[:-1]):
        cols = slice(index * PAIR, (index + 1) * PAIR)
        out_ref[:, :, cols] = mine_ref[:, :, cols] + back_ref[...]


def local(node_features, result_cotangent, proj_weights, cluster_pairs, cluster_fill, global_nodes):
    features = node_features[0]
    cotangent = result_cotangent[0]
    pairs = cluster_pairs[0]
    fill = cluster_fill[0]
    global_ids = global_nodes[0]
    weights = jnp.transpose(proj_weights, (1, 0, 2))
    nodes, width = features.shape
    half_width = cotangent.shape[1]
    lookups = pairs.shape[1]
    shards = lax.axis_size("seq")
    reps = lax.axis_size("rep")
    me = lax.axis_index("seq")
    total = shards * nodes
    count = global_ids.shape[0]
    share = width // (shards * reps)

    def trade(value, step):
        return lax.ppermute(value, "seq", [(j, j ^ step) for j in range(shards)])

    def swap(value, axis):
        return lax.ppermute(value, axis, [(0, 1), (1, 0)])

    half = lax.dynamic_slice_in_dim(features, lax.axis_index("tp") * (nodes // 2), nodes // 2)
    steps = [1] + list(range(shards - 1, 1, -1))
    near = {step: trade(half, step) for step in steps}
    far = {1: swap(near[1], "tp")}
    dout = call(
        prepare_kernel, "prepare", total, (pairs,), (cotangent,), (shape(BF16, nodes + TAIL, half_width),),
        micros=1,
    )[0]
    douts = {0: dout, 1: trade(dout, 1)}
    ids = ((global_ids // nodes) ^ me) * nodes + global_ids % nodes
    flat = shape(BF16, nodes, half_width)
    columns = shape(BF16, reps * share, nodes)
    *first, put, pick = call(
        project_first_kernel, "project_first", total, (),
        (ids[None, :], ids[:, None], weights, features),
        (flat, flat, flat, columns, shape(BF16, total, count), shape(BF16, count, total)), micros=2,
    )
    second = call(
        project_next_kernel, "project_next", total, (), (weights, near[1], far[1]),
        (flat, flat, flat, columns), (pltpu.VMEM((nodes, width), BF16),), micros=2,
    )
    for step in steps[1:]:
        near[step], _ = lax.optimization_barrier((near[step], (first[0], second[0])))
        far[step] = swap(near[step], "tp")
        ready, _ = lax.optimization_barrier((dout, near[step]))
        douts[step] = trade(ready, step)
    q, k, v, left = call(
        functools.partial(project_kernel, shards), "project", total, (),
        (weights, pick, *first, *second, *[near[i] for i in range(2, shards)], *[far[i] for i in range(2, shards)]),
        (
            shape(BF16, total, half_width),
            shape(BF16, total + count, half_width),
            shape(BF16, total + count, half_width),
            shape(BF16, reps * share, total),
        ),
        (pltpu.VMEM((total - 2 * nodes, width), BF16),),
    )

    acc = shape(F32, total + count, half_width)
    listed = lookups * GROUP_VERTICES + count
    grid = (listed, 2 * GROUP_VERTICES)
    probs = shape(BF16, nodes // GROUP_VERTICES * (half_width // PAIR), *grid)
    scratch = tuple(pltpu.VMEM((2,) + grid, kind) for kind in (F32, F32, BF16, BF16))
    dqs = {}
    dk = dv = kept = None
    for group in [[0] + steps[:1]] + [[step] for step in steps[1:-1]]:
        first = 0 in group
        got = call(
            functools.partial(attend_kernel, group, total, lookups, first), "attend_%d" % group[-1], total,
            (fill,), (q, k, v, *[douts[i] for i in group]) + (() if first else (dk, dv)),
            (acc, acc) + ((probs,) if first else ()) + (flat,) * len(group), scratch,
        )
        dk, dv = got[:2]
        kept = got[2] if first else kept
        dqs.update(zip(group, got[-len(group) :]))
    last = steps[-1]
    other, grads = [], []
    for column in range(0, half_width, PAIR):
        final = column + PAIR == half_width
        got = call(
            functools.partial(finish_kernel, last, shards, total, lookups, column, final),
            "finish_%d" % column, total, (fill,),
            (q, douts[last], k, v, dk, dv, left, put)
            + tuple(dqs[i] for i in sorted(dqs)) + ((weights, *grads) if final else ()),
            (
                shape(F32, 3, (reps - 1) * share, PAIR),
                shape(BF16, total, 3 * PAIR),
            ) + ((shape(F32, nodes, width),) if final else ()),
            (
                pltpu.VMEM((total + count, PAIR), F32),
                pltpu.VMEM((total + count, PAIR), F32),
                pltpu.VMEM((nodes, PAIR), BF16),
            ) + scratch,
        )
        other.append(got[0])
        grads.append(got[1])
    node_part = got[2]
    back = [swap(block, "rep") for block in other] if reps == 2 else [block for block in other]
    later, _ = lax.optimization_barrier((kept, (node_part, back[:-1])))
    mixed, mine = call(
        functools.partial(mix_kernel, total, lookups), "mix", total, (fill,), (dout, v, later, left, *grads),
        (flat, shape(F32, 3, share, half_width)), micros=40,
    )

    grad_x = call(
        features_kernel, "features", total, (), (features, node_part, swap(node_part, "tp")),
        (shape(BF16, nodes, width),), micros=5,
    )[0]
    if reps == 2:
        ready, _ = lax.optimization_barrier((mine, grad_x))
        grad_w = call(
            join_kernel, "join", total, (), (ready, *back), (shape(F32, 3, share, half_width),),
        )[0]
    else:
        whole = jnp.concatenate([mine, jnp.concatenate(other, 2)], 1)
        whole = jnp.roll(whole, lax.axis_index("rep") * share, 1)
        grad_w = lax.psum_scatter(whole, "rep", scatter_dimension=1, tiled=True)
    return mixed[None], grad_x[None], jnp.transpose(grad_w, (1, 0, 2))


def solution(mesh):
    placed = (
        P(("groups", "rep"), "seq", None),
        P(("groups", "rep"), "seq", "tp"),
        P(None, None, "tp"),
        P(("groups", "rep"), "seq", None),
        P(("groups", "rep"), None),
        P(("groups", "rep"), None),
    )
    return jax.shard_map(
        local,
        mesh=mesh,
        in_specs=placed,
        out_specs=(
            P(("groups", "rep"), "seq", "tp"),
            P(("groups", "rep"), "seq", None),
            P(("groups", "seq", "rep"), None, "tp"),
        ),
        check_vma=False,
    )
```
